512 devices in a mesh: tile: 64 (over x_hi, z, core), sec: 8 (over x_lo, y).
Axes of the slice: x: 4 (x_hi: 2, x_lo: 2; x = x_hi * 2 + x_lo), y: 4, z: 16, core: 2. Of those that a mesh axis runs over, the one named last changes fastest.
Arguments:
- obj: float32 [2, 8, 8192, 256], P(None, 'sec', 'tile'), may hold values from -1.25 to 1.25, as said below
- probe: float32 [2, 4, 128, 128], replicated, may hold values from -3 to 3
- measured: float32 [128, 128, 128], P('tile'), may hold values from 0.5 to 4
- row_offset: int32 [128], P('tile'), may hold values from 0 to 127
- col_offset: int32 [128], P('tile'), may hold values from 0 to 128
Outputs:
- obj_grad: float32 [2, 8, 8192, 256], P(None, 'sec', 'tile')
- probe_grad: float32 [2, 4, 128, 128], P(None, None, 'sec')
The draws below stay inside these ranges and needn't reach their ends.
Inputs may be any that keep to these rules, and one draw needn't show every extreme that they name: `obj`: real and imaginary parts of a transmission of magnitude 0.75 to 1.25.
All inputs are finite; a program needn't handle non-finite values.
Results may differ from the reference program's by a relative error of at most 0.0003.
Values sent between devices are 32-bit elements; how exact they have to be, the bound alone decides.
No kernel may reach another device: no remote copies, remote signals or barrier semaphores. Data moves between devices by JAX's collectives and lax.ppermute only.
A program may use at most 64 MiB of HBM per device.

```python
import math
import jax
import jax.numpy as jnp
from jax import lax

M = 128
K = 4
POS_DEV = 2
OR = 128
OC = 256
SLICES = 8
ROWS = 8192
POSITIONS = 128
N_TILE = 64


def draw_obj(key, part):
    key = jax.random.fold_in(key, 11)
    key_amp, key_phase = jax.random.split(key)
    shape = (SLICES, ROWS, OC)
    amplitude = jax.random.uniform(key_amp, shape, jnp.float32, 0.8, 1.2)
    phase = jnp.clip(0.4 * jax.random.normal(key_phase, shape, jnp.float32), -1.0, 1.0)
    return jnp.stack([amplitude * jnp.cos(phase), amplitude * jnp.sin(phase)])


def place_ends(drawn, rng, low, high):
    index_at = [jax.random.randint(jax.random.fold_in(rng, axis), (), 0, length) for axis, length in enumerate(drawn.shape)]
    main_axis = drawn.shape.index(max(drawn.shape))
    neighbour = index_at[:main_axis] + [(index_at[main_axis] + 1) % drawn.shape[main_axis]] + index_at[main_axis + 1:]
    return drawn.at[tuple(index_at)].set(low).at[tuple(neighbour)].set(high)


def levels(rng, shape, cuts, least, high):
    factor_of, own = 1.0, jax.random.fold_in(rng, 6)
    for dim, shards_of in cuts:
        draws = jnp.exp(jax.random.uniform(jax.random.fold_in(own, dim), (shards_of,), jnp.float32, least / len(cuts), high / len(cuts)))
        factor_of = factor_of * jnp.repeat(draws, shape[dim] // shards_of).reshape([-1 if axis == dim else 1 for axis in range(len(shape))])
    return factor_of


def normal_values(key, shape, spread, bound, kind=jnp.bfloat16):
    array = jax.random.normal(key, shape, jnp.float32) * spread
    return jnp.minimum(jnp.maximum(array, -bound), bound).astype(kind)


def setup_inputs(seed: int = 0) -> dict:
    arg_keys = jax.random.split(jax.random.key(seed), 6)
    return {
        "obj": draw_obj(jax.random.fold_in(arg_keys[5], 71), 0),
        "probe": normal_values(arg_keys[1], (2, K, M, M), 0.5, 3.0, jnp.float32),
        "measured": jnp.clip(0.5 + 3.5 * jax.random.uniform(arg_keys[2], (POSITIONS, M, M), jnp.float32) ** levels(arg_keys[2], (POSITIONS, M, M), ((0, 64),), -0.2, 0.2), 0.5, 4.0),
        "row_offset": place_ends(jax.random.randint(arg_keys[3], (POSITIONS,), 0, OR), jax.random.fold_in(arg_keys[3], 1), 0, OR - 1).astype(jnp.int32),
        "col_offset": place_ends(jax.random.randint(arg_keys[4], (POSITIONS,), 0, OC - M + 1), jax.random.fold_in(arg_keys[4], 1), 0, OC - M).astype(jnp.int32),
    }


PHASE_RATE = 0.05
HIGH = lax.Precision.HIGHEST

def optics(size):
    index = jnp.arange(size, dtype=jnp.int32)
    product = index[:, None] * index[None, :] % size
    angle = product.astype(jnp.float32) * (2.0 * math.pi / size)
    norm_scale = 1.0 / math.sqrt(size)
    four_re = jnp.cos(angle) * norm_scale
    four_im = -jnp.sin(angle) * norm_scale
    freq = (index + size // 2) % size - size // 2
    phase = (freq * freq).astype(jnp.float32) * PHASE_RATE
    kern_re = jnp.cos(phase)
    kern_im = -jnp.sin(phase)
    scaled_re = kern_re[:, None] * four_re - kern_im[:, None] * four_im
    scaled_im = kern_re[:, None] * four_im + kern_im[:, None] * four_re
    prop_re = jnp.dot(four_re, scaled_re, precision=HIGH) + jnp.dot(four_im, scaled_im, precision=HIGH)
    prop_im = jnp.dot(four_re, scaled_im, precision=HIGH) - jnp.dot(four_im, scaled_re, precision=HIGH)
    return (four_re, four_im, prop_re, prop_im)

def left_mult(matrix, field):
    return jnp.einsum('ab,...bc->...ac', matrix, field, precision=HIGH)

def right_mult(field, matrix):
    return jnp.einsum('...ac,dc->...ad', field, matrix, precision=HIGH)

def sandwich(mat_re, mat_im, field_re, field_im):
    half_re = left_mult(mat_re, field_re) - left_mult(mat_im, field_im)
    half_im = left_mult(mat_re, field_im) + left_mult(mat_im, field_re)
    out_re = right_mult(half_re, mat_re) - right_mult(half_im, mat_im)
    out_im = right_mult(half_re, mat_im) + right_mult(half_im, mat_re)
    return (out_re, out_im)

def position_loss(windows, probe, measured_one, tables):
    four_re, four_im, prop_re, prop_im = tables
    wave_re = probe[0]
    wave_im = probe[1]
    for slice_index in range(SLICES):
        obj_re = windows[0, slice_index]
        obj_im = windows[1, slice_index]
        exit_re = wave_re * obj_re - wave_im * obj_im
        exit_im = wave_re * obj_im + wave_im * obj_re
        wave_re, wave_im = sandwich(prop_re, prop_im, exit_re, exit_im)
    far_re, far_im = sandwich(four_re, four_im, wave_re, wave_im)
    intensity = lax.optimization_barrier(jnp.sum(far_re * far_re + far_im * far_im, axis=0))
    return 0.5 * jnp.sum((intensity - measured_one) ** 2)

def reference(obj, probe, measured, row_offset, col_offset):
    tables = optics(M)
    wrapped = jnp.concatenate([obj, obj[:, :, :M]], axis=2)
    grad_fn = jax.grad(position_loss, argnums=(0, 1))
    zero_index = jnp.int32(0)

    def per_tile(probe_acc, tile_index):
        tile_rows = lax.dynamic_slice_in_dim(wrapped, (tile_index * OR).astype(jnp.int32), OR + M, 2)

        def per_position(inner, local_index):
            tile_grad, acc_probe = inner
            flat = (tile_index * POS_DEV + local_index).astype(jnp.int32)
            row_first = row_offset[flat].astype(jnp.int32)
            col_first = col_offset[flat].astype(jnp.int32)
            starts = (zero_index, zero_index, row_first, col_first)
            window = lax.dynamic_slice(tile_rows, starts, (2, SLICES, M, M))
            grad_window, grad_probe = grad_fn(window, probe, measured[flat], tables)
            before = lax.dynamic_slice(tile_grad, starts, (2, SLICES, M, M))
            tile_grad = lax.dynamic_update_slice(tile_grad, before + grad_window, starts)
            return ((tile_grad, acc_probe + grad_probe), None)
        start_state = (jnp.zeros((2, SLICES, OR + M, OC), jnp.float32), probe_acc)
        (tile_grad, probe_acc), _ = lax.scan(per_position, start_state, jnp.arange(POS_DEV, dtype=jnp.int32))
        return (probe_acc, tile_grad)
    probe_sum, tiles = lax.scan(per_tile, jnp.zeros_like(probe), jnp.arange(N_TILE, dtype=jnp.int32))
    owned = tiles[:, :, :, :OR]
    spill = tiles[:, :, :, OR:]
    owned = owned.at[:, :, :, :M].add(jnp.roll(spill, 1, axis=0))
    obj_grad = jnp.transpose(owned, (1, 2, 0, 3, 4)).reshape(2, SLICES, ROWS, OC)
    return (obj_grad, probe_sum / POSITIONS)
```

```python
import functools
import math

import jax
import jax.numpy as jnp
import ml_dtypes
import numpy as np
from jax import lax
from jax.experimental import pallas as pl
from jax.experimental.pallas import tpu as pltpu
from jax.sharding import PartitionSpec as P

PHASE_RATE = 0.05
SUBLANES = 8
AXES = ("tile", "sec")
POSITION_BIT, CORE_BIT, Z_BITS, X_BIT = 2, 3, (4, 5, 6, 7), 8


def optics(size):
    index = np.arange(size, dtype=np.int32)
    product = index[:, None] * index[None, :] % size
    angle = product.astype(np.float32) * np.float32(2.0 * math.pi / size)
    norm_scale = np.float32(1.0 / math.sqrt(size))
    four = np.cos(angle) * norm_scale - 1j * (np.sin(angle) * norm_scale)
    freq = (index + size // 2) % size - size // 2
    phase = (freq * freq).astype(np.float32) * np.float32(PHASE_RATE)
    kern = np.cos(phase.astype(np.float64)) - 1j * np.sin(phase.astype(np.float64))
    prop = np.conj(four) @ (kern[:, None] * four)
    return four, prop


def as_real(matrix):
    return np.block([[matrix.real, -matrix.imag], [matrix.imag, matrix.real]]).astype(np.float32)


def halves_of(matrix):
    high = matrix.astype(ml_dtypes.bfloat16)
    low = (matrix - high.astype(np.float32)).astype(ml_dtypes.bfloat16)
    return high, low


def tables(size):
    found = []
    for matrix in reversed(optics(size)):
        real = as_real(matrix)
        for one in (real, np.ascontiguousarray(real.T)):
            found.extend(halves_of(one))
    return found


def split(value):
    high = value.astype(jnp.bfloat16)
    low = (value - high.astype(jnp.float32)).astype(jnp.bfloat16)
    return high, low


def dot(left, right):
    return jnp.dot(left, right, preferred_element_type=jnp.float32)


def sandwich(left, right, fields):
    size = fields[0][0].shape[0]
    stacked = jnp.concatenate([jnp.concatenate(pair, axis=0) for pair in fields], axis=1)
    high, low = split(stacked)
    half = dot(left[0][...], high) + (dot(left[0][...], low) + dot(left[1][...], high))
    blocks = [half[:, k * size : (k + 1) * size] for k in range(len(fields))]
    half = jnp.concatenate(
        [jnp.concatenate([b[:size], b[size:]], axis=1) for b in blocks], axis=0
    )
    high, low = split(half)
    out = dot(high, right[0][...]) + (dot(low, right[0][...]) + dot(high, right[1][...]))
    rows = [out[k * size : (k + 1) * size] for k in range(len(fields))]
    return [(row[:, :size], row[:, size:]) for row in rows]


def wave_kernel(
    sec_ref,
    windows,
    probe,
    measured,
    prop_high,
    prop_low,
    back_high,
    back_low,
    four_high,
    four_low,
    inv_high,
    inv_low,
    own_grad,
    sent_grad,
    probe_bands,
    waves,
    grads,
    window_grads,
    probe_grad,
):
    slices = windows.shape[0]
    modes = probe.shape[1]
    size = probe.shape[-1]
    prop, back = (prop_high, prop_low), (back_high, back_low)
    four, inv = (four_high, four_low), (inv_high, inv_low)
    sec = sec_ref[0]
    half_secs = slices // 2
    waves[0] = probe[...]

    def exits(step):
        win_re, win_im = windows[step, 0], windows[step, 1]
        found = []
        for k in range(modes):
            wave_re, wave_im = waves[step, 0, k], waves[step, 1, k]
            found.append((wave_re * win_re - wave_im * win_im, wave_re * win_im + wave_im * win_re))
        return found

    def forward(step, carry):
        for k, (out_re, out_im) in enumerate(sandwich(prop, back, exits(step))):
            waves[step + 1, 0, k] = out_re
            waves[step + 1, 1, k] = out_im
        return carry

    lax.fori_loop(0, slices - 1, forward, 0)
    far = sandwich(four, inv, exits(slices - 1))
    intensity = sum(re * re + im * im for re, im in far)
    weight = 2.0 * (intensity - measured[sec // half_secs])
    for k, (re, im) in enumerate(sandwich(inv, four, [(weight * re, weight * im) for re, im in far])):
        grads[0, k] = re
        grads[1, k] = im

    def window_grad(step):
        total_re = total_im = 0.0
        for k in range(modes):
            wave_re, wave_im = waves[step, 0, k], waves[step, 1, k]
            grad_re, grad_im = grads[0, k], grads[1, k]
            total_re = total_re + (wave_re * grad_re + wave_im * grad_im)
            total_im = total_im + (wave_re * grad_im - wave_im * grad_re)
        window_grads[step, 0] = total_re
        window_grads[step, 1] = total_im

    def entering(step):
        win_re, win_im = windows[step, 0], windows[step, 1]
        found = []
        for k in range(modes):
            grad_re, grad_im = grads[0, k], grads[1, k]
            found.append((win_re * grad_re + win_im * grad_im, win_re * grad_im - win_im * grad_re))
        return found

    def backward(count, carry):
        step = slices - 1 - count
        window_grad(step)
        for k, (re, im) in enumerate(sandwich(back, prop, entering(step))):
            grads[0, k] = re
            grads[1, k] = im
        return carry

    lax.fori_loop(0, slices - 1, backward, 0)
    window_grad(0)
    for k, (re, im) in enumerate(entering(0)):
        probe_grad[k] = re
        probe_grad[modes + k] = im
    own_grad[...] = window_grads[sec]
    partner = lax.rem(sec + half_secs, slices)
    sent_grad[...] = window_grads[partner]
    band = size // slices
    for position in range(2):
        first = (position * half_secs + lax.rem(sec, half_secs)) * band
        probe_bands[position] = probe_grad[:, pl.ds(pl.multiple_of(first, band), band), :]


def aligned(row, size):
    over = lax.rem(row, SUBLANES)
    return pl.multiple_of(row - over, SUBLANES), over, size + SUBLANES


def cut_kernel(row_ref, col_ref, obj, rim, cut, extended):
    own_rows = obj.shape[1]
    size = cut.shape[-1]
    secs = cut.shape[0]
    cols = obj.shape[2]
    count = row_ref.shape[0]
    extended[:, :own_rows] = obj[...]
    extended[:, own_rows:] = rim[...]
    for position in range(count):
        row, col = row_ref[position], col_ref[position]
        base, over, taken = aligned(row, size)
        shift = lax.rem(cols - col, cols)
        for part in range(2):
            rows = extended[part, pl.ds(base, taken), :]
            rows = pltpu.roll(rows, lax.rem(taken - over, taken), 0)[:size]
            window = pltpu.roll(rows, shift, 1)[:, :size]
            for sec in range(position * secs // count, (position + 1) * secs // count):
                cut[sec, part] = window


def scatter_kernel(sec_ref, row_ref, col_ref, own_grad, other_grad, owned, spill, grid):
    rows = owned.shape[1]
    cols = owned.shape[2]
    size = own_grad.shape[-1]
    own = sec_ref[0] // (sec_ref[1] // 2)
    grid[...] = jnp.zeros_like(grid)
    for source, position in ((own_grad, own), (other_grad, 1 - own)):
        row, col = row_ref[position], col_ref[position]
        base, over, taken = aligned(row, size)
        for part in range(2):
            wide = jnp.concatenate([source[part], jnp.zeros((size, cols - size), jnp.float32)], axis=1)
            tall = jnp.concatenate([pltpu.roll(wide, col, 1), jnp.zeros((taken - size, cols), jnp.float32)], axis=0)
            grid[part, pl.ds(base, taken), :] += pltpu.roll(tall, over, 0)
    owned[...] = grid[:, :rows]
    spill[...] = grid[:, rows:]


def groups_of(bits, total):
    rest = [bit for bit in range(total) if bit not in bits]
    found = []
    for r in range(1 << len(rest)):
        base = sum(((r >> i) & 1) << bit for i, bit in enumerate(rest))
        found.append([base + sum(((m >> i) & 1) << bit for i, bit in enumerate(bits)) for m in range(1 << len(bits))])
    return found


def exchanged(blocks, bits):
    total = (lax.axis_size("tile") * lax.axis_size("sec")).bit_length() - 1
    return lax.all_to_all(blocks, AXES, 0, 0, axis_index_groups=groups_of(bits, total))


def per_device(obj, probe, measured, row_offset, col_offset):
    size = probe.shape[-1]
    modes = probe.shape[1]
    rows, cols = obj.shape[2:]
    secs, tiles = lax.axis_size("sec"), lax.axis_size("tile")
    sec = lax.axis_index("sec")
    f32 = jnp.float32
    vmem = pl.BlockSpec(memory_space=pltpu.VMEM)
    smem = pl.BlockSpec(memory_space=pltpu.SMEM)
    params = pltpu.CompilerParams(vmem_limit_bytes=48 * 1024 * 1024)

    own = obj[:, 0]
    rim = lax.ppermute(own, "tile", [(i, (i - 1) % tiles) for i in range(tiles)])
    cut = pl.pallas_call(
        cut_kernel,
        out_shape=jax.ShapeDtypeStruct((secs, 2, size, size), f32),
        in_specs=[smem, smem, vmem, vmem],
        out_specs=vmem,
        scratch_shapes=[pltpu.VMEM((2, 2 * rows, cols), f32)],
        compiler_params=params,
        name="cut_windows",
    )(row_offset, col_offset, own, rim)
    windows = lax.all_to_all(cut, "sec", 0, 0)

    constants = [jnp.asarray(table) for table in tables(size)]
    band = size // secs
    own_grad, sent_grad, bands = pl.pallas_call(
        wave_kernel,
        out_shape=(
            jax.ShapeDtypeStruct((2, size, size), f32),
            jax.ShapeDtypeStruct((2, size, size), f32),
            jax.ShapeDtypeStruct((2, 2 * modes, band, size), f32),
        ),
        in_specs=[smem] + [vmem] * (3 + len(constants)),
        out_specs=(vmem, vmem, vmem),
        scratch_shapes=[
            pltpu.VMEM((secs, 2, modes, size, size), f32),
            pltpu.VMEM((2, modes, size, size), f32),
            pltpu.VMEM((secs, 2, size, size), f32),
            pltpu.VMEM((2 * modes, size, size), f32),
        ],
        compiler_params=params,
        name="wave_gradients",
    )(sec[None], windows, probe, measured, *constants)

    half = secs // 2
    other_grad = lax.ppermute(sent_grad, "sec", [(i, (i + half) % secs) for i in range(secs)])

    near = (CORE_BIT, Z_BITS[0], X_BIT)
    arrived = exchanged(bands.reshape(-1, band, size), near + (POSITION_BIT,))
    part = jnp.sum(arrived, axis=0)

    owned, spill = pl.pallas_call(
        scatter_kernel,
        out_shape=(
            jax.ShapeDtypeStruct((2, rows, cols), f32),
            jax.ShapeDtypeStruct((2, rows, cols), f32),
        ),
        in_specs=[smem, smem, smem, vmem, vmem],
        out_specs=(vmem, vmem),
        scratch_shapes=[pltpu.VMEM((2, 2 * rows, cols), f32)],
        compiler_params=params,
        name="scatter_windows",
    )(jnp.stack([sec, jnp.int32(secs)]), row_offset, col_offset, own_grad, other_grad)
    received = lax.ppermute(spill, "tile", [(i, (i + 1) % tiles) for i in range(tiles)])

    far_bits = Z_BITS[1:]
    part = jnp.sum(exchanged(jnp.broadcast_to(part, (1 << len(far_bits),) + part.shape), far_bits), axis=0)
    pieces = exchanged(jnp.broadcast_to(part, (1 << len(near),) + part.shape), near)
    obj_grad = (owned + received)[:, None]
    probe_grad = pieces.reshape(2, modes, band, size) * (1.0 / (measured.shape[0] * tiles))
    return (obj_grad, probe_grad)


def solution(mesh):
    return jax.shard_map(
        per_device,
        mesh=mesh,
        in_specs=(P(None, "sec", "tile", None), P(), P("tile", None, None), P("tile"), P("tile")),
        out_specs=(P(None, "sec", "tile", None), P(None, None, "sec", None)),
        check_vma=False,
    )
```

```python
import functools
import math

import jax
import jax.numpy as jnp
import ml_dtypes
import numpy as np
from jax import lax
from jax.experimental import pallas as pl
from jax.experimental.pallas import tpu as pltpu
from jax.sharding import PartitionSpec as P

PHASE_RATE = 0.05
SUBLANES = 8
VMEM_BYTES = 48 * 1024 * 1024
AXES = ("tile", "sec")
POSITION_BIT, CORE_BIT, Z_BITS, X_BIT = 2, 3, (4, 5, 6, 7), 8


def optics(size):
    index = np.arange(size, dtype=np.int32)
    product = index[:, None] * index[None, :] % size
    angle = product.astype(np.float32) * np.float32(2.0 * math.pi / size)
    norm_scale = np.float32(1.0 / math.sqrt(size))
    four = np.cos(angle) * norm_scale - 1j * (np.sin(angle) * norm_scale)
    freq = (index + size // 2) % size - size // 2
    phase = (freq * freq).astype(np.float32) * np.float32(PHASE_RATE)
    kern = np.cos(phase.astype(np.float64)) - 1j * np.sin(phase.astype(np.float64))
    prop = np.conj(four) @ (kern[:, None] * four)
    return four, prop


def as_real(matrix):
    return np.block([[matrix.real, -matrix.imag], [matrix.imag, matrix.real]]).astype(np.float32)


def halves_of(matrix):
    high = matrix.astype(ml_dtypes.bfloat16)
    low = (matrix - high.astype(np.float32)).astype(ml_dtypes.bfloat16)
    return high, low


def tables(size):
    found = []
    for matrix in reversed(optics(size)):
        real = as_real(matrix)
        for one in (real, np.ascontiguousarray(real.T)):
            found.extend(halves_of(one))
    return found


def split(value):
    high = value.astype(jnp.bfloat16)
    low = (value - high.astype(jnp.float32)).astype(jnp.bfloat16)
    return high, low


def dot(left, right):
    return jnp.dot(left, right, preferred_element_type=jnp.float32)


def flipped(block):
    size = block.shape[0]
    return jnp.concatenate([block[:, :size].T, block[:, size:].T], axis=1)


def product(halves, right):
    high, low = halves
    return dot(high, right[0][...]) + (dot(low, right[0][...]) + dot(high, right[1][...]))


def sandwich(right, fields):
    first = [product(split(jnp.concatenate(pair, axis=1)), right) for pair in fields]
    turned_over = [tuple(flipped(part) for part in split(half)) for half in first]
    out = [product(halves, right) for halves in turned_over]
    size = fields[0][0].shape[0]
    return [(field[:, :size], field[:, size:]) for field in out]


def wave_kernel(
    scale,
    sec_ref,
    windows,
    probe,
    measured,
    prop_high,
    prop_low,
    back_high,
    back_low,
    four_high,
    four_low,
    inv_high,
    inv_low,
    own_grad,
    sent_grad,
    probe_bands,
    waves,
    grads,
    window_grads,
    probe_grad,
):
    slices = windows.shape[0]
    modes = probe.shape[1]
    size = probe.shape[-1]
    prop, back = (prop_high, prop_low), (back_high, back_low)
    four, inv = (four_high, four_low), (inv_high, inv_low)
    sec = sec_ref[0]
    half_secs = slices // 2
    waves[0] = probe[...]

    def exits(step):
        win_re, win_im = windows[step, 0], windows[step, 1]
        found = []
        for k in range(modes):
            wave_re, wave_im = waves[step, 0, k], waves[step, 1, k]
            found.append((wave_re * win_re - wave_im * win_im, wave_re * win_im + wave_im * win_re))
        return found

    for step in range(slices - 1):
        for k, (out_re, out_im) in enumerate(sandwich(back, exits(step))):
            waves[step + 1, 0, k] = out_re
            waves[step + 1, 1, k] = out_im
    far = sandwich(inv, exits(slices - 1))
    intensity = sum(re * re + im * im for re, im in far)
    weight = 2.0 * (intensity - measured[sec // half_secs])
    for k, (re, im) in enumerate(sandwich(four, [(weight * re, weight * im) for re, im in far])):
        grads[0, k] = re
        grads[1, k] = im

    def window_grad(step):
        total_re = total_im = 0.0
        for k in range(modes):
            wave_re, wave_im = waves[step, 0, k], waves[step, 1, k]
            grad_re, grad_im = grads[0, k], grads[1, k]
            total_re = total_re + (wave_re * grad_re + wave_im * grad_im)
            total_im = total_im + (wave_re * grad_im - wave_im * grad_re)
        window_grads[step, 0] = total_re.T if step % 2 else total_re
        window_grads[step, 1] = total_im.T if step % 2 else total_im

    def entering(step):
        win_re, win_im = windows[step, 0], windows[step, 1]
        found = []
        for k in range(modes):
            grad_re, grad_im = grads[0, k], grads[1, k]
            found.append((win_re * grad_re + win_im * grad_im, win_re * grad_im - win_im * grad_re))
        return found

    for step in reversed(range(1, slices)):
        window_grad(step)
        for k, (re, im) in enumerate(sandwich(prop, entering(step))):
            grads[0, k] = re
            grads[1, k] = im
    window_grad(0)
    for k, (re, im) in enumerate(entering(0)):
        probe_grad[k] = re * scale
        probe_grad[modes + k] = im * scale
    own_grad[...] = window_grads[sec]
    partner = lax.rem(sec + half_secs, slices)
    sent_grad[...] = window_grads[partner]
    band = size // slices
    for position in range(2):
        first = (position * half_secs + lax.rem(sec, half_secs)) * band
        probe_bands[position] = probe_grad[:, pl.ds(pl.multiple_of(first, band), band), :]


def aligned(row, size):
    over = lax.rem(row, SUBLANES)
    return pl.multiple_of(row - over, SUBLANES), over, size + SUBLANES


def turned(block, row, col, size):
    rows, cols = block.shape
    block = pltpu.roll(block, lax.rem(rows - row, rows), 0)
    return pltpu.roll(block, lax.rem(cols - col, cols), 1)[:, :size]


def own_kernel(row_ref, col_ref, obj, out):
    for position in range(out.shape[0]):
        for part in range(2):
            out[position, part] = turned(obj[part], row_ref[position], col_ref[position], out.shape[-1])


def cut_kernel(sec_ref, row_ref, col_ref, own, rim, cut):
    size = cut.shape[-1]
    secs = cut.shape[0]
    count = own.shape[0]
    odd = lax.rem(sec_ref[0], 2) == 1
    place = lax.broadcasted_iota(jnp.int32, (size, size), 0)
    for position in range(count):
        row = row_ref[position]
        for part in range(2):
            beyond = turned(rim[part], row, col_ref[position], size)
            window = jnp.where(place < size - row, own[position, part], beyond)
            window = jnp.where(odd, window.T, window)
            for sec in range(position * secs // count, (position + 1) * secs // count):
                cut[sec, part] = window


def scatter_kernel(sec_ref, row_ref, col_ref, own_grad, other_grad, owned, spill, grid):
    rows = owned.shape[1]
    cols = owned.shape[2]
    size = own_grad.shape[-1]
    own = sec_ref[0] // (sec_ref[1] // 2)
    grid[...] = jnp.zeros_like(grid)
    for source, position in ((own_grad, own), (other_grad, 1 - own)):
        row, col = row_ref[position], col_ref[position]
        base, over, taken = aligned(row, size)
        for part in range(2):
            wide = jnp.concatenate([source[part], jnp.zeros((size, cols - size), jnp.float32)], axis=1)
            tall = jnp.concatenate([pltpu.roll(wide, col, 1), jnp.zeros((taken - size, cols), jnp.float32)], axis=0)
            grid[part, pl.ds(base, taken), :] += pltpu.roll(tall, over, 0)
    owned[...] = grid[:, :rows]
    spill[...] = grid[:, rows:]


def groups_of(bits, total):
    rest = [bit for bit in range(total) if bit not in bits]
    found = []
    for r in range(1 << len(rest)):
        base = sum(((r >> i) & 1) << bit for i, bit in enumerate(rest))
        found.append([base + sum(((m >> i) & 1) << bit for i, bit in enumerate(bits)) for m in range(1 << len(bits))])
    return found


def exchanged(blocks, bits):
    total = (lax.axis_size("tile") * lax.axis_size("sec")).bit_length() - 1
    return lax.all_to_all(blocks, AXES, 0, 0, axis_index_groups=groups_of(bits, total))


def wave_call(sec, windows, probe, measured, positions=128):
    secs = windows.shape[0]
    modes, size = probe.shape[1], probe.shape[-1]
    f32 = jnp.float32
    vmem = pl.BlockSpec(memory_space=pltpu.VMEM)
    smem = pl.BlockSpec(memory_space=pltpu.SMEM)
    constants = [jnp.asarray(table) for table in tables(size)]
    band = size // secs
    return pl.pallas_call(
        functools.partial(wave_kernel, 1.0 / positions),
        out_shape=(
            jax.ShapeDtypeStruct((2, size, size), f32),
            jax.ShapeDtypeStruct((2, size, size), f32),
            jax.ShapeDtypeStruct((2, 2 * modes, band, size), f32),
        ),
        in_specs=[smem] + [vmem] * (3 + len(constants)),
        out_specs=(vmem, vmem, vmem),
        scratch_shapes=[
            pltpu.VMEM((secs, 2, modes, size, size), f32),
            pltpu.VMEM((2, modes, size, size), f32),
            pltpu.VMEM((secs, 2, size, size), f32),
            pltpu.VMEM((2 * modes, size, size), f32),
        ],
        compiler_params=pltpu.CompilerParams(vmem_limit_bytes=VMEM_BYTES),
        name="wave_gradients",
    )(sec, windows, probe, measured, *constants)


def per_device(obj, probe, measured, row_offset, col_offset):
    size = probe.shape[-1]
    modes = probe.shape[1]
    rows, cols = obj.shape[2:]
    secs, tiles = lax.axis_size("sec"), lax.axis_size("tile")
    sec = lax.axis_index("sec")
    f32 = jnp.float32
    vmem = pl.BlockSpec(memory_space=pltpu.VMEM)
    smem = pl.BlockSpec(memory_space=pltpu.SMEM)
    params = pltpu.CompilerParams(vmem_limit_bytes=VMEM_BYTES)

    own = obj[:, 0]
    rim = lax.ppermute(own, "tile", [(i, (i - 1) % tiles) for i in range(tiles)])
    own_windows = pl.pallas_call(
        own_kernel,
        out_shape=jax.ShapeDtypeStruct((measured.shape[0], 2, size, size), f32),
        in_specs=[smem, smem, vmem],
        out_specs=vmem,
        compiler_params=params,
        name="own_windows",
    )(row_offset, col_offset, own)
    cut = pl.pallas_call(
        cut_kernel,
        out_shape=jax.ShapeDtypeStruct((secs, 2, size, size), f32),
        in_specs=[smem, smem, smem, vmem, vmem],
        out_specs=vmem,
        compiler_params=params,
        name="cut_windows",
    )(sec[None], row_offset, col_offset, own_windows, rim)
    windows = lax.all_to_all(cut, "sec", 0, 0)

    own_grad, sent_grad, bands = wave_call(sec[None], windows, probe, measured, measured.shape[0] * tiles)

    band = size // secs
    half = secs // 2
    other_grad = lax.ppermute(sent_grad, "sec", [(i, (i + half) % secs) for i in range(secs)])

    near = (CORE_BIT, Z_BITS[0], X_BIT)
    arrived = exchanged(bands.reshape(-1, band, size), near + (POSITION_BIT,))
    part = jnp.sum(arrived, axis=0)
    other_grad = lax.optimization_barrier((other_grad, part))[0]

    owned, spill = pl.pallas_call(
        scatter_kernel,
        out_shape=(
            jax.ShapeDtypeStruct((2, rows, cols), f32),
            jax.ShapeDtypeStruct((2, rows, cols), f32),
        ),
        in_specs=[smem, smem, smem, vmem, vmem],
        out_specs=(vmem, vmem),
        scratch_shapes=[pltpu.VMEM((2, 2 * rows, cols), f32)],
        compiler_params=params,
        name="scatter_windows",
    )(jnp.stack([sec, jnp.int32(secs)]), row_offset, col_offset, own_grad, other_grad)
    far_bits = Z_BITS[1:]
    part = jnp.sum(exchanged(jnp.broadcast_to(part, (1 << len(far_bits),) + part.shape), far_bits), axis=0)
    spill = lax.optimization_barrier((spill, part))[0]
    received = lax.ppermute(spill, "tile", [(i, (i + 1) % tiles) for i in range(tiles)])

    pieces = exchanged(jnp.broadcast_to(part, (1 << len(near),) + part.shape), near)
    obj_grad = (owned + received)[:, None]
    probe_grad = pieces.reshape(2, modes, band, size)
    return (obj_grad, probe_grad)


def solution(mesh):
    return jax.shard_map(
        per_device,
        mesh=mesh,
        in_specs=(P(None, "sec", "tile", None), P(), P("tile", None, None), P("tile"), P("tile")),
        out_specs=(P(None, "sec", "tile", None), P(None, None, "sec", None)),
        check_vma=False,
    )
```

```python
import functools
import math

import jax
import jax.numpy as jnp
import ml_dtypes
import numpy as np
from jax import lax
from jax.experimental import pallas as pl
from jax.experimental.pallas import tpu as pltpu
from jax.sharding import PartitionSpec as P

PHASE_RATE = 0.05
SUBLANES = 8
VMEM_BYTES = 48 * 1024 * 1024
SUM_COST = 100 * 1000 * 1000
AXES = ("tile", "sec")
POSITION_BIT, CORE_BIT, Z_BITS, X_BIT = 2, 3, (4, 5, 6, 7), 8


def optics(size):
    index = np.arange(size, dtype=np.int32)
    product = index[:, None] * index[None, :] % size
    angle = product.astype(np.float32) * np.float32(2.0 * math.pi / size)
    norm_scale = np.float32(1.0 / math.sqrt(size))
    four = np.cos(angle) * norm_scale - 1j * (np.sin(angle) * norm_scale)
    freq = (index + size // 2) % size - size // 2
    phase = (freq * freq).astype(np.float32) * np.float32(PHASE_RATE)
    kern = np.cos(phase.astype(np.float64)) - 1j * np.sin(phase.astype(np.float64))
    prop = np.conj(four) @ (kern[:, None] * four)
    return four, prop


def as_real(matrix):
    return np.block([[matrix.real, -matrix.imag], [matrix.imag, matrix.real]]).astype(np.float32)


def halves_of(matrix):
    high = matrix.astype(ml_dtypes.bfloat16)
    low = (matrix - high.astype(np.float32)).astype(ml_dtypes.bfloat16)
    return high, low


def tables(size):
    found = []
    for matrix in reversed(optics(size)):
        real = as_real(matrix)
        for one in (real, np.ascontiguousarray(real.T)):
            found.extend(halves_of(one))
    return found


def split(value):
    high = value.astype(jnp.bfloat16)
    low = (value - high.astype(jnp.float32)).astype(jnp.bfloat16)
    return high, low


def dot(left, right):
    return jnp.dot(left, right, preferred_element_type=jnp.float32)


def flipped(block):
    size = block.shape[0]
    return jnp.concatenate([block[:, :size].T, block[:, size:].T], axis=1)


def product(halves, right):
    high, low = halves
    return dot(high, right[0][...]) + (dot(low, right[0][...]) + dot(high, right[1][...]))


def sandwich(right, fields):
    first = [product(split(jnp.concatenate(pair, axis=1)), right) for pair in fields]
    turned_over = [split(flipped(half)) for half in first]
    out = [product(halves, right) for halves in turned_over]
    size = fields[0][0].shape[0]
    return [(field[:, :size], field[:, size:]) for field in out]


def wave_kernel(
    scale,
    sec_ref,
    windows,
    probe,
    measured,
    prop_high,
    prop_low,
    back_high,
    back_low,
    four_high,
    four_low,
    inv_high,
    inv_low,
    own_grad,
    sent_grad,
    probe_bands,
    waves,
    grads,
    window_grads,
    probe_grad,
):
    slices = windows.shape[0]
    modes = probe.shape[1]
    size = probe.shape[-1]
    prop, back = (prop_high, prop_low), (back_high, back_low)
    four, inv = (four_high, four_low), (inv_high, inv_low)
    sec = sec_ref[0]
    half_secs = slices // 2
    waves[0] = probe[...]

    def exits(step):
        win_re, win_im = windows[step, 0], windows[step, 1]
        found = []
        for k in range(modes):
            wave_re, wave_im = waves[step, 0, k], waves[step, 1, k]
            found.append((wave_re * win_re - wave_im * win_im, wave_re * win_im + wave_im * win_re))
        return found

    for step in range(slices - 1):
        for k, (out_re, out_im) in enumerate(sandwich(back, exits(step))):
            waves[step + 1, 0, k] = out_re
            waves[step + 1, 1, k] = out_im
    far = sandwich(inv, exits(slices - 1))
    intensity = sum(re * re + im * im for re, im in far)
    weight = 2.0 * (intensity - measured[sec // half_secs])
    for k, (re, im) in enumerate(sandwich(four, [(weight * re, weight * im) for re, im in far])):
        grads[0, k] = re
        grads[1, k] = im

    def window_grad(step):
        total_re = total_im = 0.0
        for k in range(modes):
            wave_re, wave_im = waves[step, 0, k], waves[step, 1, k]
            grad_re, grad_im = grads[0, k], grads[1, k]
            total_re = total_re + (wave_re * grad_re + wave_im * grad_im)
            total_im = total_im + (wave_re * grad_im - wave_im * grad_re)
        window_grads[step, 0] = total_re.T if step % 2 else total_re
        window_grads[step, 1] = total_im.T if step % 2 else total_im

    def entering(step):
        win_re, win_im = windows[step, 0], windows[step, 1]
        found = []
        for k in range(modes):
            grad_re, grad_im = grads[0, k], grads[1, k]
            found.append((win_re * grad_re + win_im * grad_im, win_re * grad_im - win_im * grad_re))
        return found

    for step in reversed(range(1, slices)):
        window_grad(step)
        for k, (re, im) in enumerate(sandwich(prop, entering(step))):
            grads[0, k] = re
            grads[1, k] = im
    window_grad(0)
    for k, (re, im) in enumerate(entering(0)):
        probe_grad[k] = re * scale
        probe_grad[modes + k] = im * scale
    own_grad[...] = window_grads[sec]
    partner = lax.rem(sec + half_secs, slices)
    sent_grad[...] = window_grads[partner]
    band = size // slices
    for position in range(2):
        first = (position * half_secs + lax.rem(sec, half_secs)) * band
        probe_bands[position] = probe_grad[:, pl.ds(pl.multiple_of(first, band), band), :]


def aligned(row, size):
    over = lax.rem(row, SUBLANES)
    return pl.multiple_of(row - over, SUBLANES), over, size + SUBLANES


def turned(block, row, col, size):
    rows, cols = block.shape
    block = pltpu.roll(block, lax.rem(rows - row, rows), 0)
    return pltpu.roll(block, lax.rem(cols - col, cols), 1)[:, :size]


def own_kernel(row_ref, col_ref, obj, out):
    for position in range(out.shape[0]):
        for part in range(2):
            out[position, part] = turned(obj[part], row_ref[position], col_ref[position], out.shape[-1])


def cut_kernel(sec_ref, row_ref, col_ref, own, rim, cut):
    size = cut.shape[-1]
    secs = cut.shape[0]
    count = own.shape[0]
    odd = lax.rem(sec_ref[0], 2) == 1
    place = lax.broadcasted_iota(jnp.int32, (size, size), 0)
    for position in range(count):
        row = row_ref[position]
        for part in range(2):
            beyond = turned(rim[part], row, col_ref[position], size)
            window = jnp.where(place < size - row, own[position, part], beyond)
            window = jnp.where(odd, window.T, window)
            for sec in range(position * secs // count, (position + 1) * secs // count):
                cut[sec, part] = window


def scatter_kernel(sec_ref, row_ref, col_ref, own_grad, other_grad, owned, spill, grid):
    rows = owned.shape[1]
    cols = owned.shape[2]
    size = own_grad.shape[-1]
    own = sec_ref[0] // (sec_ref[1] // 2)
    grid[...] = jnp.zeros_like(grid)
    for source, position in ((own_grad, own), (other_grad, 1 - own)):
        row, col = row_ref[position], col_ref[position]
        base, over, taken = aligned(row, size)
        for part in range(2):
            wide = jnp.concatenate([source[part], jnp.zeros((size, cols - size), jnp.float32)], axis=1)
            tall = jnp.concatenate([pltpu.roll(wide, col, 1), jnp.zeros((taken - size, cols), jnp.float32)], axis=0)
            grid[part, pl.ds(base, taken), :] += pltpu.roll(tall, over, 0)
    owned[...] = grid[:, :rows]
    spill[...] = grid[:, rows:]


def finish_kernel(owned, received, pieces, obj_grad, probe_grad):
    obj_grad[:, 0] = owned[...] + received[...]
    probe_grad[...] = pieces[...]


def spread_kernel(blocks, out):
    total = blocks[0]
    for k in range(1, blocks.shape[0]):
        total = total + blocks[k]
    for k in range(out.shape[0]):
        out[k] = total


def summed_to(blocks, count, name):
    return pl.pallas_call(
        spread_kernel,
        out_shape=jax.ShapeDtypeStruct((count,) + blocks.shape[1:], blocks.dtype),
        in_specs=[pl.BlockSpec(memory_space=pltpu.VMEM)],
        out_specs=pl.BlockSpec(memory_space=pltpu.VMEM),
        compiler_params=pltpu.CompilerParams(vmem_limit_bytes=VMEM_BYTES),
        cost_estimate=pl.CostEstimate(flops=0, bytes_accessed=SUM_COST, transcendentals=0),
        name=name,
    )(blocks)


def groups_of(bits, total):
    rest = [bit for bit in range(total) if bit not in bits]
    found = []
    for r in range(1 << len(rest)):
        base = sum(((r >> i) & 1) << bit for i, bit in enumerate(rest))
        found.append([base + sum(((m >> i) & 1) << bit for i, bit in enumerate(bits)) for m in range(1 << len(bits))])
    return found


def exchanged(blocks, bits):
    total = (lax.axis_size("tile") * lax.axis_size("sec")).bit_length() - 1
    return lax.all_to_all(blocks, AXES, 0, 0, axis_index_groups=groups_of(bits, total))


def wave_call(sec, windows, probe, measured, positions=128):
    secs = windows.shape[0]
    modes, size = probe.shape[1], probe.shape[-1]
    f32 = jnp.float32
    vmem = pl.BlockSpec(memory_space=pltpu.VMEM)
    smem = pl.BlockSpec(memory_space=pltpu.SMEM)
    constants = [jnp.asarray(table) for table in tables(size)]
    band = size // secs
    return pl.pallas_call(
        functools.partial(wave_kernel, 1.0 / positions),
        out_shape=(
            jax.ShapeDtypeStruct((2, size, size), f32),
            jax.ShapeDtypeStruct((2, size, size), f32),
            jax.ShapeDtypeStruct((2, 2 * modes, band, size), f32),
        ),
        in_specs=[smem] + [vmem] * (3 + len(constants)),
        out_specs=(vmem, vmem, vmem),
        scratch_shapes=[
            pltpu.VMEM((secs, 2, modes, size, size), f32),
            pltpu.VMEM((2, modes, size, size), f32),
            pltpu.VMEM((secs, 2, size, size), f32),
            pltpu.VMEM((2 * modes, size, size), f32),
        ],
        compiler_params=pltpu.CompilerParams(vmem_limit_bytes=VMEM_BYTES),
        name="wave_gradients",
    )(sec, windows, probe, measured, *constants)


def per_device(obj, probe, measured, row_offset, col_offset):
    size = probe.shape[-1]
    modes = probe.shape[1]
    rows, cols = obj.shape[2:]
    secs, tiles = lax.axis_size("sec"), lax.axis_size("tile")
    sec = lax.axis_index("sec")
    f32 = jnp.float32
    vmem = pl.BlockSpec(memory_space=pltpu.VMEM)
    smem = pl.BlockSpec(memory_space=pltpu.SMEM)
    params = pltpu.CompilerParams(vmem_limit_bytes=VMEM_BYTES)

    own = obj[:, 0]
    rim = lax.ppermute(own, "tile", [(i, (i - 1) % tiles) for i in range(tiles)])
    own_windows = pl.pallas_call(
        own_kernel,
        out_shape=jax.ShapeDtypeStruct((measured.shape[0], 2, size, size), f32),
        in_specs=[smem, smem, vmem],
        out_specs=vmem,
        compiler_params=params,
        name="own_windows",
    )(row_offset, col_offset, own)
    cut = pl.pallas_call(
        cut_kernel,
        out_shape=jax.ShapeDtypeStruct((secs, 2, size, size), f32),
        in_specs=[smem, smem, smem, vmem, vmem],
        out_specs=vmem,
        compiler_params=params,
        name="cut_windows",
    )(sec[None], row_offset, col_offset, own_windows, rim)
    windows = lax.all_to_all(cut, "sec", 0, 0)

    own_grad, sent_grad, bands = wave_call(sec[None], windows, probe, measured, measured.shape[0] * tiles)

    band = size // secs
    half = secs // 2
    other_grad = lax.ppermute(sent_grad, "sec", [(i, (i + half) % secs) for i in range(secs)])

    near, far = (CORE_BIT, Z_BITS[0], X_BIT), Z_BITS[1:]
    arrived = exchanged(bands.reshape(-1, band, size), near + (POSITION_BIT,))
    part = summed_to(arrived, 1 << len(far), "sum_near")
    other_grad = lax.optimization_barrier((other_grad, part))[0]
    arrived = exchanged(part, far)

    owned, spill = pl.pallas_call(
        scatter_kernel,
        out_shape=(
            jax.ShapeDtypeStruct((2, rows, cols), f32),
            jax.ShapeDtypeStruct((2, rows, cols), f32),
        ),
        in_specs=[smem, smem, smem, vmem, vmem],
        out_specs=(vmem, vmem),
        scratch_shapes=[pltpu.VMEM((2, 2 * rows, cols), f32)],
        compiler_params=params,
        name="scatter_windows",
    )(jnp.stack([sec, jnp.int32(secs)]), row_offset, col_offset, own_grad, other_grad)
    received = lax.ppermute(spill, "tile", [(i, (i + 1) % tiles) for i in range(tiles)])

    pieces = exchanged(summed_to(arrived, 1 << len(near), "sum_far"), near)
    return pl.pallas_call(
        finish_kernel,
        out_shape=(
            jax.ShapeDtypeStruct((2, 1, rows, cols), f32),
            jax.ShapeDtypeStruct((2, modes, band, size), f32),
        ),
        in_specs=[vmem, vmem, vmem],
        out_specs=(vmem, vmem),
        compiler_params=params,
        name="finish",
    )(owned, received, pieces.reshape(2, modes, band, size))


def solution(mesh):
    return jax.shard_map(
        per_device,
        mesh=mesh,
        in_specs=(P(None, "sec", "tile", None), P(), P("tile", None, None), P("tile"), P("tile")),
        out_specs=(P(None, "sec", "tile", None), P(None, None, "sec", None)),
        check_vma=False,
    )
```

```python
import functools
import math

import jax
import jax.numpy as jnp
import ml_dtypes
import numpy as np
from jax import lax
from jax.experimental import pallas as pl
from jax.experimental.pallas import tpu as pltpu
from jax.sharding import PartitionSpec as P

PHASE_RATE = 0.05
ORDER = (0, 6, 3, 5, 1, 7, 2, 4)
SUBLANES = 8
VMEM_BYTES = 48 * 1024 * 1024
SUM_COST = 100 * 1000 * 1000
AXES = ("tile", "sec")
POSITION_BIT, CORE_BIT, Z_BITS, X_BIT = 2, 3, (4, 5, 6, 7), 8


def optics(size):
    index = np.arange(size, dtype=np.int32)
    product = index[:, None] * index[None, :] % size
    angle = product.astype(np.float32) * np.float32(2.0 * math.pi / size)
    norm_scale = np.float32(1.0 / math.sqrt(size))
    four = np.cos(angle) * norm_scale - 1j * (np.sin(angle) * norm_scale)
    freq = (index + size // 2) % size - size // 2
    phase = (freq * freq).astype(np.float32) * np.float32(PHASE_RATE)
    kern = np.cos(phase.astype(np.float64)) - 1j * np.sin(phase.astype(np.float64))
    prop = np.conj(four) @ (kern[:, None] * four)
    return four, prop


def as_real(matrix):
    return np.block([[matrix.real, -matrix.imag], [matrix.imag, matrix.real]]).astype(np.float32)


def halves_of(matrix):
    high = matrix.astype(ml_dtypes.bfloat16)
    low = (matrix - high.astype(np.float32)).astype(ml_dtypes.bfloat16)
    return high, low


def tables(size):
    found = []
    for matrix in reversed(optics(size)):
        real = as_real(matrix)
        for one in (real, np.ascontiguousarray(real.T)):
            found.extend(halves_of(one))
    return found


def split(value):
    high = value.astype(jnp.bfloat16)
    low = (value - high.astype(jnp.float32)).astype(jnp.bfloat16)
    return high, low


def dot(left, right):
    return jnp.dot(left, right, preferred_element_type=jnp.float32)


def flipped(block):
    size = block.shape[0]
    return jnp.concatenate([block[:, :size].T, block[:, size:].T], axis=1)


def product(halves, right):
    high, low = halves
    tall = dot(jnp.concatenate([high, low], axis=0), right[0][...])
    return tall[: high.shape[0]] + (tall[high.shape[0] :] + dot(high, right[1][...]))


def sandwich(right, fields):
    first = [product(split(jnp.concatenate(pair, axis=1)), right) for pair in fields]
    turned_over = [split(flipped(half)) for half in first]
    out = [product(halves, right) for halves in turned_over]
    size = fields[0][0].shape[0]
    return [(field[:, :size], field[:, size:]) for field in out]


def wave_kernel(
    scale,
    sec_ref,
    windows,
    probe,
    measured,
    prop_high,
    prop_low,
    back_high,
    back_low,
    four_high,
    four_low,
    inv_high,
    inv_low,
    own_grad,
    sent_grad,
    probe_bands,
    waves,
    grads,
    window_grads,
    probe_grad,
):
    slices = windows.shape[0]
    modes = probe.shape[1]
    size = probe.shape[-1]
    prop, back = (prop_high, prop_low), (back_high, back_low)
    four, inv = (four_high, four_low), (inv_high, inv_low)
    sec = sec_ref[0]
    half_secs = slices // 2
    waves[0] = probe[...]

    def exits(step):
        win_re, win_im = windows[ORDER.index(step), 0], windows[ORDER.index(step), 1]
        found = []
        for k in range(modes):
            wave_re, wave_im = waves[step, 0, k], waves[step, 1, k]
            found.append((wave_re * win_re - wave_im * win_im, wave_re * win_im + wave_im * win_re))
        return found

    for step in range(slices - 1):
        for k, (out_re, out_im) in enumerate(sandwich(back, exits(step))):
            waves[step + 1, 0, k] = out_re
            waves[step + 1, 1, k] = out_im
    far = sandwich(inv, exits(slices - 1))
    intensity = sum(re * re + im * im for re, im in far)
    weight = 2.0 * (intensity - measured[sec // half_secs])
    for k, (re, im) in enumerate(sandwich(four, [(weight * re, weight * im) for re, im in far])):
        grads[0, k] = re
        grads[1, k] = im

    def window_grad(step):
        total_re = total_im = 0.0
        for k in range(modes):
            wave_re, wave_im = waves[step, 0, k], waves[step, 1, k]
            grad_re, grad_im = grads[0, k], grads[1, k]
            total_re = total_re + (wave_re * grad_re + wave_im * grad_im)
            total_im = total_im + (wave_re * grad_im - wave_im * grad_re)
        window_grads[step, 0] = total_re.T if step % 2 else total_re
        window_grads[step, 1] = total_im.T if step % 2 else total_im

    def entering(step):
        win_re, win_im = windows[ORDER.index(step), 0], windows[ORDER.index(step), 1]
        found = []
        for k in range(modes):
            grad_re, grad_im = grads[0, k], grads[1, k]
            found.append((win_re * grad_re + win_im * grad_im, win_re * grad_im - win_im * grad_re))
        return found

    for step in reversed(range(1, slices)):
        window_grad(step)
        for k, (re, im) in enumerate(sandwich(prop, entering(step))):
            grads[0, k] = re
            grads[1, k] = im
    window_grad(0)
    for k, (re, im) in enumerate(entering(0)):
        probe_grad[k] = re * scale
        probe_grad[modes + k] = im * scale
    own_grad[...] = window_grads[sec]
    partner = lax.rem(sec + half_secs, slices)
    sent_grad[...] = window_grads[partner]
    band = size // slices
    for position in range(2):
        first = (position * half_secs + lax.rem(sec, half_secs)) * band
        probe_bands[position] = probe_grad[:, pl.ds(pl.multiple_of(first, band), band), :]


def aligned(row, size):
    over = lax.rem(row, SUBLANES)
    return pl.multiple_of(row - over, SUBLANES), over, size + SUBLANES


def turned(block, row, col, size):
    rows, cols = block.shape
    block = pltpu.roll(block, lax.rem(rows - row, rows), 0)
    return pltpu.roll(block, lax.rem(cols - col, cols), 1)[:, :size]


def own_kernel(row_ref, col_ref, obj, out):
    for position in range(out.shape[0]):
        for part in range(2):
            out[position, part] = turned(obj[part], row_ref[position], col_ref[position], out.shape[-1])


def cut_kernel(sec_ref, row_ref, col_ref, own, rim, cut):
    size = cut.shape[-1]
    secs = cut.shape[0]
    count = own.shape[0]
    odd = lax.rem(sec_ref[0], 2) == 1
    place = lax.broadcasted_iota(jnp.int32, (size, size), 0)
    for position in range(count):
        row = row_ref[position]
        for part in range(2):
            beyond = turned(rim[part], row, col_ref[position], size)
            window = jnp.where(place < size - row, own[position, part], beyond)
            window = jnp.where(odd, window.T, window)
            for sec in range(position * secs // count, (position + 1) * secs // count):
                cut[ORDER.index(sec), part] = window


def scatter_kernel(sec_ref, row_ref, col_ref, own_grad, other_grad, owned, spill, grid):
    rows = owned.shape[1]
    cols = owned.shape[2]
    size = own_grad.shape[-1]
    own = sec_ref[0] // (sec_ref[1] // 2)
    grid[...] = jnp.zeros_like(grid)
    for source, position in ((own_grad, own), (other_grad, 1 - own)):
        row, col = row_ref[position], col_ref[position]
        base, over, taken = aligned(row, size)
        for part in range(2):
            wide = jnp.concatenate([source[part], jnp.zeros((size, cols - size), jnp.float32)], axis=1)
            tall = jnp.concatenate([pltpu.roll(wide, col, 1), jnp.zeros((taken - size, cols), jnp.float32)], axis=0)
            grid[part, pl.ds(base, taken), :] += pltpu.roll(tall, over, 0)
    owned[...] = grid[:, :rows]
    spill[...] = grid[:, rows:]


def finish_kernel(owned, received, pieces, obj_grad, probe_grad):
    obj_grad[:, 0] = owned[...] + received[...]
    probe_grad[...] = pieces[...]


def spread_kernel(blocks, out):
    total = blocks[0]
    for k in range(1, blocks.shape[0]):
        total = total + blocks[k]
    for k in range(out.shape[0]):
        out[k] = total


def summed_to(blocks, count, name):
    return pl.pallas_call(
        spread_kernel,
        out_shape=jax.ShapeDtypeStruct((count,) + blocks.shape[1:], blocks.dtype),
        in_specs=[pl.BlockSpec(memory_space=pltpu.VMEM)],
        out_specs=pl.BlockSpec(memory_space=pltpu.VMEM),
        compiler_params=pltpu.CompilerParams(vmem_limit_bytes=VMEM_BYTES),
        cost_estimate=pl.CostEstimate(flops=0, bytes_accessed=SUM_COST, transcendentals=0),
        name=name,
    )(blocks)


def groups_of(bits, total):
    rest = [bit for bit in range(total) if bit not in bits]
    found = []
    for r in range(1 << len(rest)):
        base = sum(((r >> i) & 1) << bit for i, bit in enumerate(rest))
        found.append([base + sum(((m >> i) & 1) << bit for i, bit in enumerate(bits)) for m in range(1 << len(bits))])
    return found


def exchanged(blocks, bits):
    total = (lax.axis_size("tile") * lax.axis_size("sec")).bit_length() - 1
    return lax.all_to_all(blocks, AXES, 0, 0, axis_index_groups=groups_of(bits, total))


def wave_call(sec, windows, probe, measured, positions=128):
    secs = windows.shape[0]
    modes, size = probe.shape[1], probe.shape[-1]
    f32 = jnp.float32
    vmem = pl.BlockSpec(memory_space=pltpu.VMEM)
    smem = pl.BlockSpec(memory_space=pltpu.SMEM)
    constants = [jnp.asarray(table) for table in tables(size)]
    band = size // secs
    return pl.pallas_call(
        functools.partial(wave_kernel, 1.0 / positions),
        out_shape=(
            jax.ShapeDtypeStruct((2, size, size), f32),
            jax.ShapeDtypeStruct((2, size, size), f32),
            jax.ShapeDtypeStruct((2, 2 * modes, band, size), f32),
        ),
        in_specs=[smem] + [vmem] * (3 + len(constants)),
        out_specs=(vmem, vmem, vmem),
        scratch_shapes=[
            pltpu.VMEM((secs, 2, modes, size, size), f32),
            pltpu.VMEM((2, modes, size, size), f32),
            pltpu.VMEM((secs, 2, size, size), f32),
            pltpu.VMEM((2 * modes, size, size), f32),
        ],
        compiler_params=pltpu.CompilerParams(vmem_limit_bytes=VMEM_BYTES),
        name="wave_gradients",
    )(sec, windows, probe, measured, *constants)


def per_device(obj, probe, measured, row_offset, col_offset):
    size = probe.shape[-1]
    modes = probe.shape[1]
    rows, cols = obj.shape[2:]
    secs, tiles = lax.axis_size("sec"), lax.axis_size("tile")
    sec = lax.axis_index("sec")
    f32 = jnp.float32
    vmem = pl.BlockSpec(memory_space=pltpu.VMEM)
    smem = pl.BlockSpec(memory_space=pltpu.SMEM)
    params = pltpu.CompilerParams(vmem_limit_bytes=VMEM_BYTES)

    own = obj[:, 0]
    rim = lax.ppermute(own, "tile", [(i, (i - 1) % tiles) for i in range(tiles)])
    own_windows = pl.pallas_call(
        own_kernel,
        out_shape=jax.ShapeDtypeStruct((measured.shape[0], 2, size, size), f32),
        in_specs=[smem, smem, vmem],
        out_specs=vmem,
        compiler_params=params,
        name="own_windows",
    )(row_offset, col_offset, own)
    cut = pl.pallas_call(
        cut_kernel,
        out_shape=jax.ShapeDtypeStruct((secs, 2, size, size), f32),
        in_specs=[smem, smem, smem, vmem, vmem],
        out_specs=vmem,
        compiler_params=params,
        name="cut_windows",
    )(sec[None], row_offset, col_offset, own_windows, rim)
    ranks = [[tile * secs + place for place in ORDER] for tile in range(tiles)]
    windows = lax.all_to_all(cut, AXES, 0, 0, axis_index_groups=ranks)

    own_grad, sent_grad, bands = wave_call(sec[None], windows, probe, measured, measured.shape[0] * tiles)

    band = size // secs
    half = secs // 2
    other_grad = lax.ppermute(sent_grad, "sec", [(i, (i + half) % secs) for i in range(secs)])

    near, far = (CORE_BIT, Z_BITS[0], X_BIT), Z_BITS[:0:-1]
    arrived = exchanged(bands.reshape(-1, band, size), near + (POSITION_BIT,))
    part = summed_to(arrived, 1 << len(far), "sum_near")
    other_grad = lax.optimization_barrier((other_grad, part))[0]
    arrived = exchanged(part, far)

    owned, spill = pl.pallas_call(
        scatter_kernel,
        out_shape=(
            jax.ShapeDtypeStruct((2, rows, cols), f32),
            jax.ShapeDtypeStruct((2, rows, cols), f32),
        ),
        in_specs=[smem, smem, smem, vmem, vmem],
        out_specs=(vmem, vmem),
        scratch_shapes=[pltpu.VMEM((2, 2 * rows, cols), f32)],
        compiler_params=params,
        name="scatter_windows",
    )(jnp.stack([sec, jnp.int32(secs)]), row_offset, col_offset, own_grad, other_grad)
    received = lax.ppermute(spill, "tile", [(i, (i + 1) % tiles) for i in range(tiles)])

    pieces = exchanged(summed_to(arrived, 1 << len(near), "sum_far"), near)
    return pl.pallas_call(
        finish_kernel,
        out_shape=(
            jax.ShapeDtypeStruct((2, 1, rows, cols), f32),
            jax.ShapeDtypeStruct((2, modes, band, size), f32),
        ),
        in_specs=[vmem, vmem, vmem],
        out_specs=(vmem, vmem),
        compiler_params=params,
        name="finish",
    )(owned, received, pieces.reshape(2, modes, band, size))


def solution(mesh):
    return jax.shard_map(
        per_device,
        mesh=mesh,
        in_specs=(P(None, "sec", "tile", None), P(), P("tile", None, None), P("tile"), P("tile")),
        out_specs=(P(None, "sec", "tile", None), P(None, None, "sec", None)),
        check_vma=False,
    )
```

```python
import functools
import math

import jax
import jax.numpy as jnp
import ml_dtypes
import numpy as np
from jax import lax
from jax.experimental import pallas as pl
from jax.experimental.pallas import tpu as pltpu
from jax.sharding import PartitionSpec as P

PHASE_RATE = 0.05
ORDER = (7, 1, 4, 2, 6, 0, 5, 3)
SUBLANES = 8
VMEM_BYTES = 48 * 1024 * 1024
SUM_COST = 100 * 1000 * 1000
AXES = ("tile", "sec")
POSITION_BIT, CORE_BIT, Z_BITS, X_BIT = 2, 3, (4, 5, 6, 7), 8


def optics(size):
    index = np.arange(size, dtype=np.int32)
    product = index[:, None] * index[None, :] % size
    angle = product.astype(np.float32) * np.float32(2.0 * math.pi / size)
    norm_scale = np.float32(1.0 / math.sqrt(size))
    four = np.cos(angle) * norm_scale - 1j * (np.sin(angle) * norm_scale)
    freq = (index + size // 2) % size - size // 2
    phase = (freq * freq).astype(np.float32) * np.float32(PHASE_RATE)
    kern = np.cos(phase.astype(np.float64)) - 1j * np.sin(phase.astype(np.float64))
    prop = np.conj(four) @ (kern[:, None] * four)
    return four, prop


def as_real(matrix):
    return np.block([[matrix.real, -matrix.imag], [matrix.imag, matrix.real]]).astype(np.float32)


def halves_of(matrix):
    high = matrix.astype(ml_dtypes.bfloat16)
    low = (matrix - high.astype(np.float32)).astype(ml_dtypes.bfloat16)
    return high, low


def tables(size):
    found = []
    for matrix in reversed(optics(size)):
        real = as_real(matrix)
        for one in (real, np.ascontiguousarray(real.T)):
            found.extend(halves_of(one))
    return found


def split(value):
    high = value.astype(jnp.bfloat16)
    low = (value - high.astype(jnp.float32)).astype(jnp.bfloat16)
    return high, low


def dot(left, right):
    return jnp.dot(left, right, preferred_element_type=jnp.float32)


def flipped(block):
    size = block.shape[0]
    return jnp.concatenate([block[:, :size].T, block[:, size:].T], axis=1)


def product(halves, right):
    high, low = halves
    tall = dot(jnp.concatenate([high, low], axis=0), right[0][...])
    return tall[: high.shape[0]] + (tall[high.shape[0] :] + dot(high, right[1][...]))


def sandwich(right, fields):
    first = [product(split(jnp.concatenate(pair, axis=1)), right) for pair in fields]
    turned_over = [split(flipped(half)) for half in first]
    out = [product(halves, right) for halves in turned_over]
    size = fields[0][0].shape[0]
    return [(field[:, :size], field[:, size:]) for field in out]


def wave_kernel(
    scale,
    sec_ref,
    windows,
    probe,
    measured,
    prop_high,
    prop_low,
    back_high,
    back_low,
    four_high,
    four_low,
    inv_high,
    inv_low,
    own_grad,
    sent_grad,
    probe_bands,
    waves,
    grads,
    window_grads,
    probe_grad,
):
    slices = windows.shape[0]
    modes = probe.shape[1]
    size = probe.shape[-1]
    prop, back = (prop_high, prop_low), (back_high, back_low)
    four, inv = (four_high, four_low), (inv_high, inv_low)
    sec = sec_ref[0]
    half_secs = slices // 2
    waves[0] = probe[...]

    def exits(step):
        win_re, win_im = windows[ORDER.index(step), 0], windows[ORDER.index(step), 1]
        found = []
        for k in range(modes):
            wave_re, wave_im = waves[step, 0, k], waves[step, 1, k]
            found.append((wave_re * win_re - wave_im * win_im, wave_re * win_im + wave_im * win_re))
        return found

    for step in range(slices - 1):
        for k, (out_re, out_im) in enumerate(sandwich(back, exits(step))):
            waves[step + 1, 0, k] = out_re
            waves[step + 1, 1, k] = out_im
    far = sandwich(inv, exits(slices - 1))
    intensity = sum(re * re + im * im for re, im in far)
    weight = 2.0 * (intensity - measured[sec // half_secs])
    for k, (re, im) in enumerate(sandwich(four, [(weight * re, weight * im) for re, im in far])):
        grads[0, k] = re
        grads[1, k] = im

    def window_grad(step):
        total_re = total_im = 0.0
        for k in range(modes):
            wave_re, wave_im = waves[step, 0, k], waves[step, 1, k]
            grad_re, grad_im = grads[0, k], grads[1, k]
            total_re = total_re + (wave_re * grad_re + wave_im * grad_im)
            total_im = total_im + (wave_re * grad_im - wave_im * grad_re)
        window_grads[step, 0] = total_re.T if step % 2 else total_re
        window_grads[step, 1] = total_im.T if step % 2 else total_im

    def entering(step):
        win_re, win_im = windows[ORDER.index(step), 0], windows[ORDER.index(step), 1]
        found = []
        for k in range(modes):
            grad_re, grad_im = grads[0, k], grads[1, k]
            found.append((win_re * grad_re + win_im * grad_im, win_re * grad_im - win_im * grad_re))
        return found

    for step in reversed(range(1, slices)):
        window_grad(step)
        for k, (re, im) in enumerate(sandwich(prop, entering(step))):
            grads[0, k] = re
            grads[1, k] = im
    window_grad(0)
    for k, (re, im) in enumerate(entering(0)):
        probe_grad[k] = re * scale
        probe_grad[modes + k] = im * scale
    own_grad[...] = window_grads[sec]
    partner = lax.rem(sec + half_secs, slices)
    sent_grad[...] = window_grads[partner]
    band = size // slices
    for position in range(2):
        first = (position * half_secs + lax.rem(sec, half_secs)) * band
        for k in range(2 * modes):
            taken = probe_grad[k, pl.ds(pl.multiple_of(first, band), band), :]
            probe_bands[1 - position, 2 * modes - 1 - k] = taken


def aligned(row, size):
    over = lax.rem(row, SUBLANES)
    return pl.multiple_of(row - over, SUBLANES), over, size + SUBLANES


def turned(block, row, col, size):
    rows, cols = block.shape
    block = pltpu.roll(block, lax.rem(rows - row, rows), 0)
    return pltpu.roll(block, lax.rem(cols - col, cols), 1)[:, :size]


def own_kernel(row_ref, col_ref, obj, out):
    for position in range(out.shape[0]):
        for part in range(2):
            out[position, part] = turned(obj[part], row_ref[position], col_ref[position], out.shape[-1])


def cut_kernel(sec_ref, row_ref, col_ref, own, rim, cut):
    size = cut.shape[-1]
    secs = cut.shape[0]
    count = own.shape[0]
    odd = lax.rem(sec_ref[0], 2) == 1
    place = lax.broadcasted_iota(jnp.int32, (size, size), 0)
    for position in range(count):
        row = row_ref[position]
        for part in range(2):
            beyond = turned(rim[part], row, col_ref[position], size)
            window = jnp.where(place < size - row, own[position, part], beyond)
            window = jnp.where(odd, window.T, window)
            for sec in range(position * secs // count, (position + 1) * secs // count):
                cut[ORDER.index(sec), part] = window


def scatter_kernel(sec_ref, row_ref, col_ref, own_grad, other_grad, owned, spill, grid):
    rows = owned.shape[1]
    cols = owned.shape[2]
    size = own_grad.shape[-1]
    own = sec_ref[0] // (sec_ref[1] // 2)
    grid[...] = jnp.zeros_like(grid)
    for source, position in ((own_grad, own), (other_grad, 1 - own)):
        row, col = row_ref[position], col_ref[position]
        base, over, taken = aligned(row, size)
        for part in range(2):
            wide = jnp.concatenate([source[part], jnp.zeros((size, cols - size), jnp.float32)], axis=1)
            tall = jnp.concatenate([pltpu.roll(wide, col, 1), jnp.zeros((taken - size, cols), jnp.float32)], axis=0)
            grid[part, pl.ds(base, taken), :] += pltpu.roll(tall, over, 0)
    owned[...] = grid[:, :rows]
    spill[...] = grid[:, rows:]


def finish_kernel(owned, received, pieces, obj_grad, probe_grad):
    obj_grad[:, 0] = owned[...] + received[...]
    count, modes = pieces.shape[0], probe_grad.shape[1]
    for k in range(count):
        probe_grad[k // modes, k % modes] = pieces[count - 1 - k]


def spread_kernel(blocks, out):
    total = blocks[0]
    for k in range(1, blocks.shape[0]):
        total = total + blocks[k]
    for k in range(out.shape[0]):
        out[k] = total


def summed_to(blocks, count, name):
    return pl.pallas_call(
        spread_kernel,
        out_shape=jax.ShapeDtypeStruct((count,) + blocks.shape[1:], blocks.dtype),
        in_specs=[pl.BlockSpec(memory_space=pltpu.VMEM)],
        out_specs=pl.BlockSpec(memory_space=pltpu.VMEM),
        compiler_params=pltpu.CompilerParams(vmem_limit_bytes=VMEM_BYTES),
        cost_estimate=pl.CostEstimate(flops=0, bytes_accessed=SUM_COST, transcendentals=0),
        name=name,
    )(blocks)


def groups_of(bits, total):
    rest = [bit for bit in range(total) if bit not in bits]
    found = []
    for r in range(1 << len(rest)):
        base = sum(((r >> i) & 1) << bit for i, bit in enumerate(rest))
        found.append([base + sum(((m >> i) & 1) << bit for i, bit in enumerate(bits)) for m in range(1 << len(bits))])
    return found


def exchanged(blocks, bits, last_first=True):
    total = (lax.axis_size("tile") * lax.axis_size("sec")).bit_length() - 1
    groups = groups_of(bits, total)
    if last_first:
        groups = [group[::-1] for group in groups]
    return lax.all_to_all(blocks, AXES, 0, 0, axis_index_groups=groups)


def wave_call(sec, windows, probe, measured, positions=128):
    secs = windows.shape[0]
    modes, size = probe.shape[1], probe.shape[-1]
    f32 = jnp.float32
    vmem = pl.BlockSpec(memory_space=pltpu.VMEM)
    smem = pl.BlockSpec(memory_space=pltpu.SMEM)
    constants = [jnp.asarray(table) for table in tables(size)]
    band = size // secs
    return pl.pallas_call(
        functools.partial(wave_kernel, 1.0 / positions),
        out_shape=(
            jax.ShapeDtypeStruct((2, size, size), f32),
            jax.ShapeDtypeStruct((2, size, size), f32),
            jax.ShapeDtypeStruct((2, 2 * modes, band, size), f32),
        ),
        in_specs=[smem] + [vmem] * (3 + len(constants)),
        out_specs=(vmem, vmem, vmem),
        scratch_shapes=[
            pltpu.VMEM((secs, 2, modes, size, size), f32),
            pltpu.VMEM((2, modes, size, size), f32),
            pltpu.VMEM((secs, 2, size, size), f32),
            pltpu.VMEM((2 * modes, size, size), f32),
        ],
        compiler_params=pltpu.CompilerParams(vmem_limit_bytes=VMEM_BYTES),
        name="wave_gradients",
    )(sec, windows, probe, measured, *constants)


def per_device(obj, probe, measured, row_offset, col_offset):
    size = probe.shape[-1]
    modes = probe.shape[1]
    rows, cols = obj.shape[2:]
    secs, tiles = lax.axis_size("sec"), lax.axis_size("tile")
    sec = lax.axis_index("sec")
    f32 = jnp.float32
    vmem = pl.BlockSpec(memory_space=pltpu.VMEM)
    smem = pl.BlockSpec(memory_space=pltpu.SMEM)
    params = pltpu.CompilerParams(vmem_limit_bytes=VMEM_BYTES)

    own = obj[:, 0]
    rim = lax.ppermute(own, "tile", [(i, (i - 1) % tiles) for i in range(tiles)])
    own_windows = pl.pallas_call(
        own_kernel,
        out_shape=jax.ShapeDtypeStruct((measured.shape[0], 2, size, size), f32),
        in_specs=[smem, smem, vmem],
        out_specs=vmem,
        compiler_params=params,
        name="own_windows",
    )(row_offset, col_offset, own)
    cut = pl.pallas_call(
        cut_kernel,
        out_shape=jax.ShapeDtypeStruct((secs, 2, size, size), f32),
        in_specs=[smem, smem, smem, vmem, vmem],
        out_specs=vmem,
        compiler_params=params,
        name="cut_windows",
    )(sec[None], row_offset, col_offset, own_windows, rim)
    ranks = [[tile * secs + place for place in ORDER] for tile in range(tiles)]
    windows = lax.all_to_all(cut, AXES, 0, 0, axis_index_groups=ranks)

    own_grad, sent_grad, bands = wave_call(sec[None], windows, probe, measured, measured.shape[0] * tiles)

    band = size // secs
    half = secs // 2
    other_grad = lax.ppermute(sent_grad, "sec", [(i, (i + half) % secs) for i in range(secs)])

    near, far = (CORE_BIT, Z_BITS[0], X_BIT), Z_BITS[1:]
    arrived = exchanged(bands.reshape(-1, band, size), near + (POSITION_BIT,))
    part = summed_to(arrived, 1 << len(far), "sum_near")
    other_grad = lax.optimization_barrier((other_grad, part))[0]
    arrived = exchanged(part, far)

    owned, spill = pl.pallas_call(
        scatter_kernel,
        out_shape=(
            jax.ShapeDtypeStruct((2, rows, cols), f32),
            jax.ShapeDtypeStruct((2, rows, cols), f32),
        ),
        in_specs=[smem, smem, smem, vmem, vmem],
        out_specs=(vmem, vmem),
        scratch_shapes=[pltpu.VMEM((2, 2 * rows, cols), f32)],
        compiler_params=params,
        name="scatter_windows",
    )(jnp.stack([sec, jnp.int32(secs)]), row_offset, col_offset, own_grad, other_grad)
    received = lax.ppermute(spill, "tile", [(i, (i + 1) % tiles) for i in range(tiles)])

    pieces = exchanged(summed_to(arrived, 1 << len(near), "sum_far"), near)
    return pl.pallas_call(
        finish_kernel,
        out_shape=(
            jax.ShapeDtypeStruct((2, 1, rows, cols), f32),
            jax.ShapeDtypeStruct((2, modes, band, size), f32),
        ),
        in_specs=[vmem, vmem, vmem],
        out_specs=(vmem, vmem),
        compiler_params=params,
        name="finish",
    )(owned, received, pieces)


def solution(mesh):
    return jax.shard_map(
        per_device,
        mesh=mesh,
        in_specs=(P(None, "sec", "tile", None), P(), P("tile", None, None), P("tile"), P("tile")),
        out_specs=(P(None, "sec", "tile", None), P(None, None, "sec", None)),
        check_vma=False,
    )
```

```python
import functools
import math

import jax
import jax.numpy as jnp
import ml_dtypes
import numpy as np
from jax import lax
from jax.experimental import pallas as pl
from jax.experimental.pallas import tpu as pltpu
from jax.sharding import PartitionSpec as P

PHASE_RATE = 0.05
ORDER = (7, 6, 5, 4, 3, 2, 1, 0)
SUBLANES = 8
VMEM_BYTES = 48 * 1024 * 1024
SUM_COST = 100 * 1000 * 1000
AXES = ("tile", "sec")
POSITION_BIT, CORE_BIT, Z_BITS, X_BIT = 2, 3, (4, 5, 6, 7), 8


def optics(size):
    index = np.arange(size, dtype=np.int32)
    product = index[:, None] * index[None, :] % size
    angle = product.astype(np.float32) * np.float32(2.0 * math.pi / size)
    norm_scale = np.float32(1.0 / math.sqrt(size))
    four = np.cos(angle) * norm_scale - 1j * (np.sin(angle) * norm_scale)
    freq = (index + size // 2) % size - size // 2
    phase = (freq * freq).astype(np.float32) * np.float32(PHASE_RATE)
    kern = np.cos(phase.astype(np.float64)) - 1j * np.sin(phase.astype(np.float64))
    prop = np.conj(four) @ (kern[:, None] * four)
    return four, prop


def as_real(matrix):
    return np.block([[matrix.real, -matrix.imag], [matrix.imag, matrix.real]]).astype(np.float32)


def halves_of(matrix):
    high = matrix.astype(ml_dtypes.bfloat16)
    low = (matrix - high.astype(np.float32)).astype(ml_dtypes.bfloat16)
    return high, low


def tables(size):
    found = []
    for matrix in reversed(optics(size)):
        real = as_real(matrix)
        for one in (real, np.ascontiguousarray(real.T)):
            found.extend(halves_of(one))
    return found


def split(value):
    high = value.astype(jnp.bfloat16)
    low = (value - high.astype(jnp.float32)).astype(jnp.bfloat16)
    return high, low


def dot(left, right):
    return jnp.dot(left, right, preferred_element_type=jnp.float32)


def flipped(block):
    size = block.shape[0]
    return jnp.concatenate([block[:, :size].T, block[:, size:].T], axis=1)


def product(halves, right):
    high, low = halves
    tall = dot(jnp.concatenate([high, low], axis=0), right[0][...])
    return tall[: high.shape[0]] + (tall[high.shape[0] :] + dot(high, right[1][...]))


def sandwich(right, fields):
    first = [product(split(jnp.concatenate(pair, axis=1)), right) for pair in fields]
    turned_over = [split(flipped(half)) for half in first]
    out = [product(halves, right) for halves in turned_over]
    size = fields[0][0].shape[0]
    return [(field[:, :size], field[:, size:]) for field in out]


def wave_kernel(
    scale,
    sec_ref,
    windows,
    probe,
    measured,
    prop_high,
    prop_low,
    back_high,
    back_low,
    four_high,
    four_low,
    inv_high,
    inv_low,
    own_grad,
    sent_grad,
    probe_bands,
    waves,
    grads,
    window_grads,
    probe_grad,
):
    slices = windows.shape[0]
    modes = probe.shape[1]
    size = probe.shape[-1]
    prop, back = (prop_high, prop_low), (back_high, back_low)
    four, inv = (four_high, four_low), (inv_high, inv_low)
    sec = sec_ref[0]
    half_secs = slices // 2
    waves[0] = probe[...]

    def exits(step):
        win_re, win_im = windows[ORDER.index(step), 0], windows[ORDER.index(step), 1]
        found = []
        for k in range(modes):
            wave_re, wave_im = waves[step, 0, k], waves[step, 1, k]
            found.append((wave_re * win_re - wave_im * win_im, wave_re * win_im + wave_im * win_re))
        return found

    for step in range(slices - 1):
        for k, (out_re, out_im) in enumerate(sandwich(back, exits(step))):
            waves[step + 1, 0, k] = out_re
            waves[step + 1, 1, k] = out_im
    far = sandwich(inv, exits(slices - 1))
    intensity = sum(re * re + im * im for re, im in far)
    weight = 2.0 * (intensity - measured[sec // half_secs])
    for k, (re, im) in enumerate(sandwich(four, [(weight * re, weight * im) for re, im in far])):
        grads[0, k] = re
        grads[1, k] = im

    def window_grad(step):
        total_re = total_im = 0.0
        for k in range(modes):
            wave_re, wave_im = waves[step, 0, k], waves[step, 1, k]
            grad_re, grad_im = grads[0, k], grads[1, k]
            total_re = total_re + (wave_re * grad_re + wave_im * grad_im)
            total_im = total_im + (wave_re * grad_im - wave_im * grad_re)
        window_grads[step, 0] = total_re.T if step % 2 else total_re
        window_grads[step, 1] = total_im.T if step % 2 else total_im

    def entering(step):
        win_re, win_im = windows[ORDER.index(step), 0], windows[ORDER.index(step), 1]
        found = []
        for k in range(modes):
            grad_re, grad_im = grads[0, k], grads[1, k]
            found.append((win_re * grad_re + win_im * grad_im, win_re * grad_im - win_im * grad_re))
        return found

    for step in reversed(range(1, slices)):
        window_grad(step)
        for k, (re, im) in enumerate(sandwich(prop, entering(step))):
            grads[0, k] = re
            grads[1, k] = im
    window_grad(0)
    for k, (re, im) in enumerate(entering(0)):
        probe_grad[k] = re * scale
        probe_grad[modes + k] = im * scale
    own_grad[...] = window_grads[sec]
    partner = lax.rem(sec + half_secs, slices)
    sent_grad[...] = window_grads[partner]
    band = size // slices
    for position in range(2):
        first = (position * half_secs + lax.rem(sec, half_secs)) * band
        for k in range(2 * modes):
            taken = probe_grad[k, pl.ds(pl.multiple_of(first, band), band), :]
            probe_bands[1 - position, 2 * modes - 1 - k] = taken


def aligned(row, size):
    over = lax.rem(row, SUBLANES)
    return pl.multiple_of(row - over, SUBLANES), over, size + SUBLANES


def turned(block, row, col, size):
    rows, cols = block.shape
    block = pltpu.roll(block, lax.rem(rows - row, rows), 0)
    return pltpu.roll(block, lax.rem(cols - col, cols), 1)[:, :size]


def own_kernel(row_ref, col_ref, obj, out):
    for position in range(out.shape[0]):
        for part in range(2):
            out[position, part] = turned(obj[part], row_ref[position], col_ref[position], out.shape[-1])


def cut_kernel(sec_ref, row_ref, col_ref, own, rim, cut):
    size = cut.shape[-1]
    secs = cut.shape[0]
    count = own.shape[0]
    odd = lax.rem(sec_ref[0], 2) == 1
    place = lax.broadcasted_iota(jnp.int32, (size, size), 0)
    for position in range(count):
        row = row_ref[position]
        for part in range(2):
            beyond = turned(rim[part], row, col_ref[position], size)
            window = jnp.where(place < size - row, own[position, part], beyond)
            window = jnp.where(odd, window.T, window)
            for sec in range(position * secs // count, (position + 1) * secs // count):
                cut[ORDER.index(sec), part] = window


def scatter_kernel(sec_ref, row_ref, col_ref, own_grad, other_grad, owned, spill, grid):
    rows = owned.shape[1]
    cols = owned.shape[2]
    size = own_grad.shape[-1]
    own = sec_ref[0] // (sec_ref[1] // 2)
    grid[...] = jnp.zeros_like(grid)
    for source, position in ((own_grad, own), (other_grad, 1 - own)):
        row, col = row_ref[position], col_ref[position]
        base, over, taken = aligned(row, size)
        for part in range(2):
            wide = jnp.concatenate([source[part], jnp.zeros((size, cols - size), jnp.float32)], axis=1)
            tall = jnp.concatenate([pltpu.roll(wide, col, 1), jnp.zeros((taken - size, cols), jnp.float32)], axis=0)
            grid[part, pl.ds(base, taken), :] += pltpu.roll(tall, over, 0)
    owned[...] = grid[:, :rows]
    spill[...] = grid[:, rows:]


def finish_kernel(owned, received, pieces, obj_grad, probe_grad):
    obj_grad[:, 0] = owned[...] + received[...]
    count, modes = pieces.shape[0], probe_grad.shape[1]
    for k in range(count):
        probe_grad[k // modes, k % modes] = pieces[count - 1 - (k ^ 1)]


def spread_kernel(blocks, out):
    total = blocks[0]
    for k in range(1, blocks.shape[0]):
        total = total + blocks[k]
    for k in range(out.shape[0]):
        out[k] = total


def summed_to(blocks, count, name):
    return pl.pallas_call(
        spread_kernel,
        out_shape=jax.ShapeDtypeStruct((count,) + blocks.shape[1:], blocks.dtype),
        in_specs=[pl.BlockSpec(memory_space=pltpu.VMEM)],
        out_specs=pl.BlockSpec(memory_space=pltpu.VMEM),
        compiler_params=pltpu.CompilerParams(vmem_limit_bytes=VMEM_BYTES),
        cost_estimate=pl.CostEstimate(flops=0, bytes_accessed=SUM_COST, transcendentals=0),
        name=name,
    )(blocks)


def groups_of(bits, total):
    rest = [bit for bit in range(total) if bit not in bits]
    found = []
    for r in range(1 << len(rest)):
        base = sum(((r >> i) & 1) << bit for i, bit in enumerate(rest))
        found.append([base + sum(((m >> i) & 1) << bit for i, bit in enumerate(bits)) for m in range(1 << len(bits))])
    return found


def exchanged(blocks, bits, flip=0):
    total = (lax.axis_size("tile") * lax.axis_size("sec")).bit_length() - 1
    groups = groups_of(bits, total)
    groups = [[group[place ^ flip] for place in reversed(range(len(group)))] for group in groups]
    return lax.all_to_all(blocks, AXES, 0, 0, axis_index_groups=groups)


def wave_call(sec, windows, probe, measured, positions=128):
    secs = windows.shape[0]
    modes, size = probe.shape[1], probe.shape[-1]
    f32 = jnp.float32
    vmem = pl.BlockSpec(memory_space=pltpu.VMEM)
    smem = pl.BlockSpec(memory_space=pltpu.SMEM)
    constants = [jnp.asarray(table) for table in tables(size)]
    band = size // secs
    return pl.pallas_call(
        functools.partial(wave_kernel, 1.0 / positions),
        out_shape=(
            jax.ShapeDtypeStruct((2, size, size), f32),
            jax.ShapeDtypeStruct((2, size, size), f32),
            jax.ShapeDtypeStruct((2, 2 * modes, band, size), f32),
        ),
        in_specs=[smem] + [vmem] * (3 + len(constants)),
        out_specs=(vmem, vmem, vmem),
        scratch_shapes=[
            pltpu.VMEM((secs, 2, modes, size, size), f32),
            pltpu.VMEM((2, modes, size, size), f32),
            pltpu.VMEM((secs, 2, size, size), f32),
            pltpu.VMEM((2 * modes, size, size), f32),
        ],
        compiler_params=pltpu.CompilerParams(vmem_limit_bytes=VMEM_BYTES),
        name="wave_gradients",
    )(sec, windows, probe, measured, *constants)


def per_device(obj, probe, measured, row_offset, col_offset):
    size = probe.shape[-1]
    modes = probe.shape[1]
    rows, cols = obj.shape[2:]
    secs, tiles = lax.axis_size("sec"), lax.axis_size("tile")
    sec = lax.axis_index("sec")
    f32 = jnp.float32
    vmem = pl.BlockSpec(memory_space=pltpu.VMEM)
    smem = pl.BlockSpec(memory_space=pltpu.SMEM)
    params = pltpu.CompilerParams(vmem_limit_bytes=VMEM_BYTES)

    own = obj[:, 0]
    rim = lax.ppermute(own, "tile", [(i, (i - 1) % tiles) for i in range(tiles)])
    own_windows = pl.pallas_call(
        own_kernel,
        out_shape=jax.ShapeDtypeStruct((measured.shape[0], 2, size, size), f32),
        in_specs=[smem, smem, vmem],
        out_specs=vmem,
        compiler_params=params,
        name="own_windows",
    )(row_offset, col_offset, own)
    cut = pl.pallas_call(
        cut_kernel,
        out_shape=jax.ShapeDtypeStruct((secs, 2, size, size), f32),
        in_specs=[smem, smem, smem, vmem, vmem],
        out_specs=vmem,
        compiler_params=params,
        name="cut_windows",
    )(sec[None], row_offset, col_offset, own_windows, rim)
    ranks = [[tile * secs + place for place in ORDER] for tile in range(tiles)]
    windows = lax.all_to_all(cut, AXES, 0, 0, axis_index_groups=ranks)

    own_grad, sent_grad, bands = wave_call(sec[None], windows, probe, measured, measured.shape[0] * tiles)

    band = size // secs
    half = secs // 2
    other_grad = lax.ppermute(sent_grad, "sec", [(i, (i + half) % secs) for i in range(secs)])

    near, far = (CORE_BIT, Z_BITS[0], X_BIT), Z_BITS[1:]
    arrived = exchanged(bands.reshape(-1, band, size), near + (POSITION_BIT,))
    part = summed_to(arrived, 1 << len(far), "sum_near")
    other_grad = lax.optimization_barrier((other_grad, part))[0]
    arrived = exchanged(part, far)

    owned, spill = pl.pallas_call(
        scatter_kernel,
        out_shape=(
            jax.ShapeDtypeStruct((2, rows, cols), f32),
            jax.ShapeDtypeStruct((2, rows, cols), f32),
        ),
        in_specs=[smem, smem, smem, vmem, vmem],
        out_specs=(vmem, vmem),
        scratch_shapes=[pltpu.VMEM((2, 2 * rows, cols), f32)],
        compiler_params=params,
        name="scatter_windows",
    )(jnp.stack([sec, jnp.int32(secs)]), row_offset, col_offset, own_grad, other_grad)
    received = lax.ppermute(spill, "tile", [(i, (i + 1) % tiles) for i in range(tiles)])

    pieces = exchanged(summed_to(arrived, 1 << len(near), "sum_far"), near, 1)
    return pl.pallas_call(
        finish_kernel,
        out_shape=(
            jax.ShapeDtypeStruct((2, 1, rows, cols), f32),
            jax.ShapeDtypeStruct((2, modes, band, size), f32),
        ),
        in_specs=[vmem, vmem, vmem],
        out_specs=(vmem, vmem),
        compiler_params=params,
        name="finish",
    )(owned, received, pieces)


def solution(mesh):
    return jax.shard_map(
        per_device,
        mesh=mesh,
        in_specs=(P(None, "sec", "tile", None), P(), P("tile", None, None), P("tile"), P("tile")),
        out_specs=(P(None, "sec", "tile", None), P(None, None, "sec", None)),
        check_vma=False,
    )
```

```python
import functools
import math

import jax
import jax.numpy as jnp
import ml_dtypes
import numpy as np
from jax import lax
from jax.experimental import pallas as pl
from jax.experimental.pallas import tpu as pltpu
from jax.sharding import PartitionSpec as P

PHASE_RATE = 0.05
ORDER = (7, 6, 5, 4, 3, 2, 1, 0)
SUBLANES = 8
VMEM_BYTES = 48 * 1024 * 1024
SUM_COST = 100 * 1000 * 1000
AXES = ("tile", "sec")
POSITION_BIT, CORE_BIT, Z_BITS, X_BIT = 2, 3, (4, 5, 6, 7), 8


def optics(size):
    index = np.arange(size, dtype=np.int32)
    product = index[:, None] * index[None, :] % size
    angle = product.astype(np.float32) * np.float32(2.0 * math.pi / size)
    norm_scale = np.float32(1.0 / math.sqrt(size))
    four = np.cos(angle) * norm_scale - 1j * (np.sin(angle) * norm_scale)
    freq = (index + size // 2) % size - size // 2
    phase = (freq * freq).astype(np.float32) * np.float32(PHASE_RATE)
    kern = np.cos(phase.astype(np.float64)) - 1j * np.sin(phase.astype(np.float64))
    prop = np.conj(four) @ (kern[:, None] * four)
    return four, prop


def as_real(matrix):
    return np.block([[matrix.real, -matrix.imag], [matrix.imag, matrix.real]]).astype(np.float32)


def halves_of(matrix):
    high = matrix.astype(ml_dtypes.bfloat16)
    low = (matrix - high.astype(np.float32)).astype(ml_dtypes.bfloat16)
    return high, low


def tables(size):
    found = []
    for matrix in reversed(optics(size)):
        real = as_real(matrix)
        for one in (real, np.ascontiguousarray(real.T)):
            found.extend(halves_of(one))
    return found


def split(value):
    high = value.astype(jnp.bfloat16)
    low = (value - high.astype(jnp.float32)).astype(jnp.bfloat16)
    return high, low


def dot(left, right):
    return jnp.dot(left, right, preferred_element_type=jnp.float32)


def flipped(block):
    size = block.shape[0]
    return jnp.concatenate([block[:, :size].T, block[:, size:].T], axis=1)


def product(halves, right):
    high, low = halves
    tall = dot(jnp.concatenate([high, low], axis=0), right[0][...])
    return tall[: high.shape[0]] + (tall[high.shape[0] :] + dot(high, right[1][...]))


def sandwich(right, fields):
    first = [product(split(jnp.concatenate(pair, axis=1)), right) for pair in fields]
    turned_over = [split(flipped(half)) for half in first]
    out = [product(halves, right) for halves in turned_over]
    size = fields[0][0].shape[0]
    return [(field[:, :size], field[:, size:]) for field in out]


def wave_kernel(
    scale,
    sec_ref,
    windows,
    probe,
    measured,
    prop_high,
    prop_low,
    back_high,
    back_low,
    four_high,
    four_low,
    inv_high,
    inv_low,
    own_grad,
    sent_grad,
    probe_bands,
    waves,
    grads,
    window_grads,
    probe_grad,
):
    slices = windows.shape[0]
    modes = probe.shape[1]
    size = probe.shape[-1]
    prop, back = (prop_high, prop_low), (back_high, back_low)
    four, inv = (four_high, four_low), (inv_high, inv_low)
    sec = sec_ref[0]
    half_secs = slices // 2

    def exits(step):
        win_re, win_im = windows[ORDER.index(step), 0], windows[ORDER.index(step), 1]
        found = []
        for k in range(modes):
            wave_re, wave_im = (waves[step, 0, k], waves[step, 1, k]) if step else (probe[0, k], probe[1, k])
            found.append((wave_re * win_re - wave_im * win_im, wave_re * win_im + wave_im * win_re))
        return found

    for step in range(slices - 1):
        for k, (out_re, out_im) in enumerate(sandwich(back, exits(step))):
            waves[step + 1, 0, k] = out_re
            waves[step + 1, 1, k] = out_im
    far = sandwich(inv, exits(slices - 1))
    intensity = sum(re * re + im * im for re, im in far)
    weight = 2.0 * (intensity - measured[sec // half_secs])
    for k, (re, im) in enumerate(sandwich(four, [(weight * re, weight * im) for re, im in far])):
        grads[0, k] = re
        grads[1, k] = im

    def window_grad(step):
        total_re = total_im = 0.0
        for k in range(modes):
            wave_re, wave_im = (waves[step, 0, k], waves[step, 1, k]) if step else (probe[0, k], probe[1, k])
            grad_re, grad_im = grads[0, k], grads[1, k]
            total_re = total_re + (wave_re * grad_re + wave_im * grad_im)
            total_im = total_im + (wave_re * grad_im - wave_im * grad_re)
        window_grads[step, 0] = total_re.T if step % 2 else total_re
        window_grads[step, 1] = total_im.T if step % 2 else total_im

    def entering(step):
        win_re, win_im = windows[ORDER.index(step), 0], windows[ORDER.index(step), 1]
        found = []
        for k in range(modes):
            grad_re, grad_im = grads[0, k], grads[1, k]
            found.append((win_re * grad_re + win_im * grad_im, win_re * grad_im - win_im * grad_re))
        return found

    for step in reversed(range(1, slices)):
        window_grad(step)
        for k, (re, im) in enumerate(sandwich(prop, entering(step))):
            grads[0, k] = re
            grads[1, k] = im
    window_grad(0)
    for k, (re, im) in enumerate(entering(0)):
        probe_grad[k] = re * scale
        probe_grad[modes + k] = im * scale
    own_grad[...] = window_grads[sec]
    partner = lax.rem(sec + half_secs, slices)
    sent_grad[...] = window_grads[partner]
    band = size // slices
    for position in range(2):
        first = (position * half_secs + lax.rem(sec, half_secs)) * band
        for k in range(2 * modes):
            taken = probe_grad[k, pl.ds(pl.multiple_of(first, band), band), :]
            probe_bands[1 - position, 2 * modes - 1 - k] = taken


def aligned(row, size):
    over = lax.rem(row, SUBLANES)
    return pl.multiple_of(row - over, SUBLANES), over, size + SUBLANES


def turned(block, row, col, size):
    rows, cols = block.shape
    block = pltpu.roll(block, lax.rem(rows - row, rows), 0)
    return pltpu.roll(block, lax.rem(cols - col, cols), 1)[:, :size]


def own_kernel(row_ref, col_ref, obj, out):
    for position in range(out.shape[0]):
        for part in range(2):
            out[position, part] = turned(obj[part], row_ref[position], col_ref[position], out.shape[-1])


def cut_kernel(sec_ref, row_ref, col_ref, own, rim, cut):
    size = cut.shape[-1]
    secs = cut.shape[0]
    count = own.shape[0]
    odd = lax.rem(sec_ref[0], 2) == 1
    place = lax.broadcasted_iota(jnp.int32, (size, size), 0)
    for position in range(count):
        row = row_ref[position]
        for part in range(2):
            beyond = turned(rim[part], row, col_ref[position], size)
            window = jnp.where(place < size - row, own[position, part], beyond)
            window = jnp.where(odd, window.T, window)
            for sec in range(position * secs // count, (position + 1) * secs // count):
                cut[ORDER.index(sec), part] = window


def scatter_kernel(sec_ref, row_ref, col_ref, own_grad, other_grad, owned, spill, grid):
    rows = owned.shape[1]
    cols = owned.shape[2]
    size = own_grad.shape[-1]
    own = sec_ref[0] // (sec_ref[1] // 2)
    grid[...] = jnp.zeros_like(grid)
    for source, position in ((own_grad, own), (other_grad, 1 - own)):
        row, col = row_ref[position], col_ref[position]
        base, over, taken = aligned(row, size)
        for part in range(2):
            wide = jnp.concatenate([source[part], jnp.zeros((size, cols - size), jnp.float32)], axis=1)
            tall = jnp.concatenate([pltpu.roll(wide, col, 1), jnp.zeros((taken - size, cols), jnp.float32)], axis=0)
            grid[part, pl.ds(base, taken), :] += pltpu.roll(tall, over, 0)
    owned[...] = grid[:, :rows]
    spill[...] = grid[:, rows:]


def finish_kernel(owned, received, pieces, obj_grad, probe_grad):
    obj_grad[:, 0] = owned[...] + received[...]
    count, modes = pieces.shape[0], probe_grad.shape[1]
    for k in range(count):
        probe_grad[k // modes, k % modes] = pieces[count - 1 - (k ^ 1)]


def spread_kernel(blocks, out):
    total = blocks[0]
    for k in range(1, blocks.shape[0]):
        total = total + blocks[k]
    for k in range(out.shape[0]):
        out[k] = total


def summed_to(blocks, count, name):
    return pl.pallas_call(
        spread_kernel,
        out_shape=jax.ShapeDtypeStruct((count,) + blocks.shape[1:], blocks.dtype),
        in_specs=[pl.BlockSpec(memory_space=pltpu.VMEM)],
        out_specs=pl.BlockSpec(memory_space=pltpu.VMEM),
        compiler_params=pltpu.CompilerParams(vmem_limit_bytes=VMEM_BYTES),
        cost_estimate=pl.CostEstimate(flops=0, bytes_accessed=SUM_COST, transcendentals=0),
        name=name,
    )(blocks)


def groups_of(bits, total):
    rest = [bit for bit in range(total) if bit not in bits]
    found = []
    for r in range(1 << len(rest)):
        base = sum(((r >> i) & 1) << bit for i, bit in enumerate(rest))
        found.append([base + sum(((m >> i) & 1) << bit for i, bit in enumerate(bits)) for m in range(1 << len(bits))])
    return found


def exchanged(blocks, bits, flip=0):
    total = (lax.axis_size("tile") * lax.axis_size("sec")).bit_length() - 1
    groups = groups_of(bits, total)
    groups = [[group[place ^ flip] for place in reversed(range(len(group)))] for group in groups]
    return lax.all_to_all(blocks, AXES, 0, 0, axis_index_groups=groups)


def wave_call(sec, windows, probe, measured, positions=128):
    secs = windows.shape[0]
    modes, size = probe.shape[1], probe.shape[-1]
    f32 = jnp.float32
    vmem = pl.BlockSpec(memory_space=pltpu.VMEM)
    smem = pl.BlockSpec(memory_space=pltpu.SMEM)
    constants = [jnp.asarray(table) for table in tables(size)]
    band = size // secs
    return pl.pallas_call(
        functools.partial(wave_kernel, 1.0 / positions),
        out_shape=(
            jax.ShapeDtypeStruct((2, size, size), f32),
            jax.ShapeDtypeStruct((2, size, size), f32),
            jax.ShapeDtypeStruct((2, 2 * modes, band, size), f32),
        ),
        in_specs=[smem] + [vmem] * (3 + len(constants)),
        out_specs=(vmem, vmem, vmem),
        scratch_shapes=[
            pltpu.VMEM((secs, 2, modes, size, size), f32),
            pltpu.VMEM((2, modes, size, size), f32),
            pltpu.VMEM((secs, 2, size, size), f32),
            pltpu.VMEM((2 * modes, size, size), f32),
        ],
        compiler_params=pltpu.CompilerParams(vmem_limit_bytes=VMEM_BYTES),
        name="wave_gradients",
    )(sec, windows, probe, measured, *constants)


def per_device(obj, probe, measured, row_offset, col_offset):
    size = probe.shape[-1]
    modes = probe.shape[1]
    rows, cols = obj.shape[2:]
    secs, tiles = lax.axis_size("sec"), lax.axis_size("tile")
    sec = lax.axis_index("sec")
    f32 = jnp.float32
    vmem = pl.BlockSpec(memory_space=pltpu.VMEM)
    smem = pl.BlockSpec(memory_space=pltpu.SMEM)
    params = pltpu.CompilerParams(vmem_limit_bytes=VMEM_BYTES)

    own = obj[:, 0]
    rim = lax.ppermute(own, "tile", [(i, (i - 1) % tiles) for i in range(tiles)])
    own_windows = pl.pallas_call(
        own_kernel,
        out_shape=jax.ShapeDtypeStruct((measured.shape[0], 2, size, size), f32),
        in_specs=[smem, smem, vmem],
        out_specs=vmem,
        compiler_params=params,
        name="own_windows",
    )(row_offset, col_offset, own)
    cut = pl.pallas_call(
        cut_kernel,
        out_shape=jax.ShapeDtypeStruct((secs, 2, size, size), f32),
        in_specs=[smem, smem, smem, vmem, vmem],
        out_specs=vmem,
        compiler_params=params,
        name="cut_windows",
    )(sec[None], row_offset, col_offset, own_windows, rim)
    ranks = [[tile * secs + place for place in ORDER] for tile in range(tiles)]
    windows = lax.all_to_all(cut, AXES, 0, 0, axis_index_groups=ranks)

    own_grad, sent_grad, bands = wave_call(sec[None], windows, probe, measured, measured.shape[0] * tiles)

    band = size // secs
    half = secs // 2
    other_grad = lax.ppermute(sent_grad, "sec", [(i, (i + half) % secs) for i in range(secs)])

    near, far = (CORE_BIT, Z_BITS[0], X_BIT), Z_BITS[1:]
    arrived = exchanged(bands.reshape(-1, band, size), near + (POSITION_BIT,))
    part = summed_to(arrived, 1 << len(far), "sum_near")
    other_grad = lax.optimization_barrier((other_grad, part))[0]
    arrived = exchanged(part, far)

    owned, spill = pl.pallas_call(
        scatter_kernel,
        out_shape=(
            jax.ShapeDtypeStruct((2, rows, cols), f32),
            jax.ShapeDtypeStruct((2, rows, cols), f32),
        ),
        in_specs=[smem, smem, smem, vmem, vmem],
        out_specs=(vmem, vmem),
        scratch_shapes=[pltpu.VMEM((2, 2 * rows, cols), f32)],
        compiler_params=params,
        name="scatter_windows",
    )(jnp.stack([sec, jnp.int32(secs)]), row_offset, col_offset, own_grad, other_grad)
    received = lax.ppermute(spill, "tile", [(i, (i + 1) % tiles) for i in range(tiles)])

    pieces = exchanged(summed_to(arrived, 1 << len(near), "sum_far"), near, 1)
    return pl.pallas_call(
        finish_kernel,
        out_shape=(
            jax.ShapeDtypeStruct((2, 1, rows, cols), f32),
            jax.ShapeDtypeStruct((2, modes, band, size), f32),
        ),
        in_specs=[vmem, vmem, vmem],
        out_specs=(vmem, vmem),
        compiler_params=params,
        name="finish",
    )(owned, received, pieces)


def solution(mesh):
    return jax.shard_map(
        per_device,
        mesh=mesh,
        in_specs=(P(None, "sec", "tile", None), P(), P("tile", None, None), P("tile"), P("tile")),
        out_specs=(P(None, "sec", "tile", None), P(None, None, "sec", None)),
        check_vma=False,
    )
```
